128 devices in a mesh: mp: 2 (over core), tx: 8 (over y, z_lo), ty: 8 (over x, z_hi).
Axes of the slice: x: 4, y: 4, z: 4 (z_hi: 2, z_lo: 2; z = z_hi * 2 + z_lo), core: 2. Of those that a mesh axis runs over, the one named last changes fastest.
Arguments:
- state: float32 [2, 16, 256, 3600], P('mp', None, 'tx', 'ty'), may hold values from -6 to 6
- diffusion: float32 [2, 256, 3600], P('mp', 'tx', 'ty'), may hold values from 0.03 to 0.22
- exchange_rate: float32 [2, 256, 3600], P('mp', 'tx', 'ty'), may hold values from 0.05 to 0.5
- land_mask: int32 [256, 3600], P('tx', 'ty'), may hold values 0 or 1
- fold_map: int32 [3600], P('ty'), may hold values from 0 to 3599, each once
- entry_tile: int32 [2, 8, 384, 1], P('mp', 'tx', 'ty'), may hold values from 0 to 63; in each aligned block of 48 rows (0 to 47, 48 to 95, ..., all dimensions but the last counted through in order) at most 3 rows name the same one
- entry_source: int32 [2, 8, 384], P('mp', 'tx', 'ty'), may hold values from 0 to 31
- entry_dest: int32 [2, 8, 384], P('mp', 'tx', 'ty'), may hold values from 0 to 31
- entry_weight: bfloat16 [2, 8, 384, 450, 450], P('mp', 'tx', 'ty'), may hold values from -0.1875 to 0.1875
Outputs:
- new_state: float32 [2, 16, 256, 3600], P('mp', None, 'tx', 'ty')
The draws below stay inside these ranges and needn't reach their ends.
Inputs may be any that keep to these rules, and one draw needn't show every extreme that they name: `entry_tile`: in each model, the blocks of one tile name each destination tile at most 3 times; some destination tile is named exactly 3 times. `fold_map`: a permutation.
All inputs are finite; a program needn't handle non-finite values. No bound on the sum of `land_mask` on one device may be relied on, other than what follows from the above.
Results may differ from the reference program's by a relative error of at most 0.0011.
Values sent between devices are 32-bit elements; how exact they have to be, the bound alone decides.
No kernel may reach another device: no remote copies, remote signals or barrier semaphores. Data moves between devices by JAX's collectives and lax.ppermute only.
A program may use at most 128 MiB of HBM per device.

```python
import math
import jax
import jax.numpy as jnp
import numpy as np
from jax import lax

LEV = 16
CX = 32
CY = 450
ENTRIES = 48
CAP = 3
NX = 256
NY = 3600
N_TX = 8
N_TY = 8


def set_ends(result, key, least, largest):
    longest = result.shape.index(max(result.shape))
    spots = []
    for shift in (0, 1):
        where = [jax.random.randint(jax.random.fold_in(key, axis), (), 0, length) for axis, length in enumerate(result.shape)]
        where[longest] = (where[longest] + shift) % result.shape[longest]
        spots.append(tuple(where))
    return result.at[spots[0]].set(least).at[spots[1]].set(largest)


def level_of(key, extent, cuts, smallest, top_value):
    level, own = 1.0, jax.random.fold_in(key, 6)
    for dim, parts in cuts:
        heights = jnp.exp(jax.random.uniform(jax.random.fold_in(own, dim), (parts,), jnp.float32, smallest / len(cuts), top_value / len(cuts)))
        level = level * jnp.repeat(heights, extent[dim] // parts).reshape([-1 if axis == dim else 1 for axis in range(len(extent))])
    return level


def deal_out(own_key, own, number, rows, amount, top, bound, lean):
    ranking = jax.random.permutation(own_key, amount)
    crowded, usual = load_shares(amount, rows * top, bound, lean, True), load_shares(amount, rows * top, bound, lean, False)
    places = jnp.arange(amount)

    def named(lengths, turn):
        used = int((lengths > 0).sum())
        fixed = max(1, used // 4)
        passed = fixed + (places - fixed + turn * (used - fixed)) % max(1, amount - fixed)
        return jnp.zeros((amount,), jnp.int32).at[ranking[jnp.where(places < fixed, places, passed)]].set(jnp.asarray(lengths, jnp.int32))

    lengths = jnp.where(number % 4 == 0, named(crowded, number // 4), named(usual, number - number // 4 - 1))
    mixed = jax.random.permutation(jax.random.fold_in(own, 3), amount)
    source_of, receiver = mixed[0:amount // 2 * 2:2], mixed[1:amount // 2 * 2:2]
    room = jnp.minimum(lengths[source_of] - 1, bound - lengths[receiver]) // 2
    room = jnp.where((source_of == ranking[0]) | (receiver == ranking[0]) | (lengths[receiver] == 0), 0, jnp.maximum(room, 0))
    passed = jax.random.randint(jax.random.fold_in(own, 4), (amount // 2,), 0, 1 << 20) % (room + 1)
    lengths = lengths.at[source_of].add(-passed).at[receiver].add(passed)
    labels = jnp.searchsorted(jnp.cumsum(lengths), jnp.arange(rows * top), side="right").astype(jnp.int32)
    table = labels.reshape(top, rows).T
    table = table[jax.random.permutation(jax.random.fold_in(own, 1), rows)]
    turn = jax.random.randint(jax.random.fold_in(own, 2), (rows, 1), 0, top)
    return jnp.take_along_axis(table, (jnp.arange(top)[None, :] + turn) % top, axis=1)


def load_shares(number_of, total, reach, slope, full):
    weights = [(1 << 20) // math.isqrt(grade ** slope) + 1 for grade in range(1, number_of + 1)]
    largest = reach if full else min(reach, max(-(-total // number_of), total * weights[0] // sum(weights)))
    least = 1 if total - largest >= number_of - 1 else 0
    counts, spare = [largest] + [least] * (number_of - 1), total - largest - least * (number_of - 1)
    while spare > 0:
        free = [i for i in range(1, number_of) if counts[i] < largest] or [i for i in range(1, number_of) if counts[i] < reach]
        pool, remaining = sum([weights[i] for i in free]), spare
        for i in free:
            extra = min(reach - counts[i], max(1, remaining * weights[i] // pool), spare)
            counts[i] = counts[i] + extra
            spare = spare - extra
    return np.array(counts)


def scatter_about(own_key, shape, deviation, limit, shards=(), kind=jnp.bfloat16):
    gain = level_of(own_key, shape, shards, -0.22, 0.18) if shards else 1.0
    drawn = jax.random.normal(own_key, shape, jnp.float32) * deviation * gain
    return jnp.minimum(jnp.maximum(drawn, -limit), limit).astype(kind)


def setup_inputs(seed: int = 0) -> dict:
    splits = jax.random.split(jax.random.key(seed), 10)
    state = scatter_about(splits[0], (2, LEV, NX, NY), 1.0, 6.0, ((0, 2), (2, 8), (3, 8)), jnp.float32)
    diffusion = jnp.clip(jnp.exp(math.log(0.22) - 1.9924302 * jax.random.uniform(splits[1], (2, NX, NY), jnp.float32) ** level_of(splits[1], (2, NX, NY), ((0, 2), (1, 8), (2, 8)), -0.2, 0.2)), 0.03, 0.22)
    exchange_rate = jnp.clip(jnp.exp(math.log(0.5) - 2.3025851 * jax.random.uniform(splits[2], (2, NX, NY), jnp.float32) ** level_of(splits[2], (2, NX, NY), ((0, 2), (1, 8), (2, 8)), -0.2, 0.2)), 0.05, 0.5)
    land_mask = set_ends((jax.random.randint(splits[3], (NX, NY), 0, 4) < 3).astype(jnp.int32), jax.random.fold_in(splits[3], 1), 0, 1)
    fold_map = jax.random.permutation(splits[4], NY).astype(jnp.int32)
    entry_tile_keys = jax.random.split(jax.random.fold_in(splits[5], 1), 2 * N_TX * (N_TY * ENTRIES) // ENTRIES)
    entry_tile_turns = jax.random.permutation(jax.random.fold_in(splits[5], 3), 2 * N_TX * (N_TY * ENTRIES) // ENTRIES)
    entry_tile = jax.vmap(lambda own, number: deal_out(jax.random.fold_in(splits[5], 2), own, number, ENTRIES, N_TX * N_TY, 1, CAP, 2))(entry_tile_keys, entry_tile_turns).reshape((2, N_TX, N_TY * ENTRIES, 1))
    entry_source = set_ends(jax.random.randint(splits[6], (2, N_TX, N_TY * ENTRIES), 0, CX), jax.random.fold_in(splits[6], 1), 0, CX - 1).astype(jnp.int32)
    entry_dest = set_ends(jax.random.randint(splits[7], (2, N_TX, N_TY * ENTRIES), 0, CX), jax.random.fold_in(splits[7], 1), 0, CX - 1).astype(jnp.int32)
    entry_weight = scatter_about(splits[8], (2, N_TX, N_TY * ENTRIES, CY, CY), (2 * CY) ** -0.5, 0.1875, ((0, 2), (1, 8), (2, 8)))
    return {"state": state, "diffusion": diffusion, "exchange_rate": exchange_rate, "land_mask": land_mask, "fold_map": fold_map, "entry_tile": entry_tile, "entry_source": entry_source, "entry_dest": entry_dest, "entry_weight": entry_weight}


def sweep(field, coef, north_row):
    zero_row = jnp.zeros_like(field[:, :1])
    above = jnp.concatenate([field[:, 1:], north_row[:, None]], axis=1)
    below = jnp.concatenate([zero_row, field[:, :-1]], axis=1)
    east = jnp.roll(field, -1, axis=2)
    west = jnp.roll(field, 1, axis=2)
    return field + coef * (above + below + east + west - 4.0 * field)


def regrid(state, entry_tile, entry_source, entry_dest, entry_weight):
    tiles = N_TX * N_TY
    sent = state.astype(jnp.bfloat16)
    blocks = sent.reshape(2, LEV, NX, N_TY, CY).transpose(0, 2, 3, 1, 4)
    tile_ids = entry_tile.reshape(2 * tiles, ENTRIES)
    sources = entry_source.reshape(2 * tiles, ENTRIES)
    targets = entry_dest.reshape(2 * tiles, ENTRIES)
    weights = entry_weight.reshape(2 * tiles, ENTRIES, CY, CY)
    order = jnp.arange(2 * tiles, dtype=jnp.int32)

    def step(total, items):
        index, tile_row, src_row, dst_row, weight = items
        model = index // tiles
        own = index % tiles
        row_tile = own // N_TY
        col_tile = own % N_TY
        pieces = blocks[model, row_tile * CX + src_row, col_tile]
        contrib = jnp.einsum("eij,elj->eli", weight.astype(jnp.float32), pieces.astype(jnp.float32),
                             precision=lax.Precision.HIGHEST)
        total = total.at[1 - model, (tile_row // N_TY) * CX + dst_row, tile_row % N_TY].add(contrib)
        return total, None

    start = jnp.zeros((2, NX, N_TY, LEV, CY), jnp.float32)
    total, unused = lax.scan(step, start, (order, tile_ids, sources, targets, weights))
    return total.transpose(0, 3, 1, 2, 4).reshape(2, LEV, NX, NY)


def reference(state, diffusion, exchange_rate, land_mask, fold_map, entry_tile, entry_source, entry_dest, entry_weight):
    received = regrid(state, entry_tile, entry_source, entry_dest, entry_weight)
    sea = land_mask.astype(jnp.float32)
    atmos = state[0]
    zero_north = jnp.zeros_like(atmos[:, 0])
    for step_number in range(2):
        atmos = sweep(atmos, diffusion[0], zero_north)
    ocean = state[1]
    ocean = sweep(ocean, diffusion[1] * sea, ocean[:, NX - 1][:, fold_map])
    atmos = atmos + exchange_rate[0] * (received[0] - state[0])
    ocean = ocean + exchange_rate[1] * sea * (received[1] - state[1])
    return jnp.stack([atmos, ocean])
```

```python
import functools

import jax
import jax.numpy as jnp
from jax import lax
from jax.experimental import pallas as pl
from jax.experimental.pallas import tpu as pltpu
from jax.sharding import PartitionSpec as P

TILE_AXES = ("tx", "ty")
QUARTERS = 4
LANES = 128
GROUP = 4
PARTS = 1
ROW_BLOCK = 256
VMEM_LIMIT = 40 * 1024 * 1024


def spans(cols):
    width = -(-cols // QUARTERS)
    return [(q * width, min(cols, (q + 1) * width)) for q in range(QUARTERS)]


def contribute_kernel(first, count, source, tile, dest, sent, weight, out):
    rows, levels, cols = sent.shape
    step = pl.program_id(0)
    lane = lax.broadcasted_iota(jnp.int32, (levels, LANES), 1)
    for g in range(GROUP):
        local = step * GROUP + g
        entry = first + local
        y = lax.dot_general(
            sent[source[entry]], weight[g], (((1,), (1,)), ((), ())), preferred_element_type=jnp.float32
        )
        tile_value = tile[entry].astype(jnp.float32)
        dest_value = dest[entry].astype(jnp.float32)
        tail = jnp.where(lane == LANES - 2, tile_value, 0.0)
        tail = jnp.where(lane == LANES - 1, dest_value, tail)
        for q, (low, high) in enumerate(spans(cols)):
            piece = jnp.concatenate([y[:, low:high], tail[:, high - low :]], axis=1)
            out[pl.ds(q * count + local, levels, stride=QUARTERS * count), :] = piece


def contribute(first, count, sent, weight, source, tile, dest):
    rows, levels, cols = sent.shape
    grid_spec = pltpu.PrefetchScalarGridSpec(
        num_scalar_prefetch=3,
        grid=(count // GROUP,),
        in_specs=[
            pl.BlockSpec((rows, levels, cols), lambda i, *_: (0, 0, 0)),
            pl.BlockSpec((GROUP, cols, cols), lambda i, *_: (first // GROUP + i, 0, 0)),
        ],
        out_specs=pl.BlockSpec((levels * QUARTERS * count, LANES), lambda i, *_: (0, 0)),
    )
    return pl.pallas_call(
        functools.partial(contribute_kernel, first, count),
        grid_spec=grid_spec,
        out_shape=jax.ShapeDtypeStruct((levels * QUARTERS * count, LANES), jnp.float32),
        compiler_params=pltpu.CompilerParams(vmem_limit_bytes=VMEM_LIMIT),
        cost_estimate=pl.CostEstimate(
            flops=2 * count * levels * cols * cols, bytes_accessed=2 * count * cols * cols, transcendentals=0
        ),
        name="contribute",
    )(source, tile, dest, sent, weight)


def gather_rows_kernel(tile_rows, values, out, halves, labels):
    block = pl.program_id(0)

    @pl.when(block == 0)
    def prepare():
        x = values[...]
        high = x.astype(jnp.bfloat16)
        low = (x - high.astype(jnp.float32)).astype(jnp.bfloat16)
        halves[:, :LANES] = high
        halves[:, LANES:] = low
        lane = lax.broadcasted_iota(jnp.int32, (8, LANES), 1)
        pick = jnp.where(lane == LANES - 2, float(tile_rows), jnp.where(lane == LANES - 1, 1.0, 0.0))
        labels[...] = lax.dot_general(
            pick.astype(jnp.bfloat16), high, (((1,), (1,)), ((), ())), preferred_element_type=jnp.float32
        ).astype(jnp.int32)

    count = values.shape[0]
    row = lax.broadcasted_iota(jnp.int32, (ROW_BLOCK, count), 0) + block * ROW_BLOCK
    onehot = jnp.where(row == labels[0:1, :], 1.0, 0.0).astype(jnp.bfloat16)
    sums = jnp.dot(onehot, halves[...], preferred_element_type=jnp.float32)
    out[...] = sums[:, :LANES] + sums[:, LANES:]


def gather_rows(values, tiles, tile_rows):
    count = values.shape[0]
    return pl.pallas_call(
        functools.partial(gather_rows_kernel, tile_rows),
        grid=(tiles * tile_rows // ROW_BLOCK,),
        in_specs=[pl.BlockSpec((count, LANES), lambda i: (0, 0))],
        out_specs=pl.BlockSpec((ROW_BLOCK, LANES), lambda i: (i, 0)),
        out_shape=jax.ShapeDtypeStruct((tiles * tile_rows, LANES), jnp.float32),
        scratch_shapes=[
            pltpu.VMEM((count, 2 * LANES), jnp.bfloat16),
            pltpu.VMEM((8, count), jnp.int32),
        ],
        compiler_params=pltpu.CompilerParams(vmem_limit_bytes=VMEM_LIMIT),
        name="gather_rows",
    )(values)


def finish_kernel(received, field, moved, rate, out):
    levels, rows, cols = field.shape
    for level in range(levels):
        parts = [
            received[level * QUARTERS + q][:, : high - low] for q, (low, high) in enumerate(spans(cols))
        ]
        whole = jnp.concatenate(parts, axis=1)
        out[level] = moved[level] + rate[...] * (whole - field[level])


def finish(received, field, moved, rate):
    return pl.pallas_call(
        finish_kernel,
        out_shape=jax.ShapeDtypeStruct(field.shape, jnp.float32),
        compiler_params=pltpu.CompilerParams(vmem_limit_bytes=VMEM_LIMIT),
        name="finish",
    )(received, field, moved, rate)


def shift(value, axis, forward, periodic):
    count = lax.axis_size(axis)
    pairs = [(i, i + 1) for i in range(count - 1)] + ([(count - 1, 0)] if periodic else [])
    if not forward:
        pairs = [(b, a) for a, b in pairs]
    return lax.ppermute(value, axis, pairs)


def sweep(f, c):
    mid = f[:, 1:-1, 1:-1]
    around = f[:, 2:, 1:-1] + f[:, :-2, 1:-1] + f[:, 1:-1, 2:] + f[:, 1:-1, :-2]
    return mid + c * (around - 4.0 * mid)


def mix(field, coef, ocean, fold_map):
    levels, rows, cols = field.shape
    stack = jnp.concatenate([field, coef[None]], axis=0)
    west = shift(stack[:, :, cols - 2 :], "ty", True, True)
    east = shift(stack[:, :, :2], "ty", False, True)
    wide = jnp.concatenate([west, stack, east], axis=2)
    south = shift(wide[:, rows - 2 :], "tx", True, False)
    north = shift(wide[:, :2], "tx", False, False)
    last = jnp.broadcast_to(field[None, :, rows - 1], (lax.axis_size("ty"), levels, cols))
    whole = lax.all_to_all(last, "ty", split_axis=0, concat_axis=0, tiled=True)
    whole = jnp.transpose(whole, (1, 0, 2)).reshape(levels, -1)
    folded = jnp.take(whole, fold_map, axis=1)
    fold_here = jnp.logical_and(ocean, lax.axis_index("tx") == lax.axis_size("tx") - 1)
    folded = jnp.pad(folded, ((0, 1), (2, 2)))
    north = jnp.concatenate([jnp.where(fold_here, folded, north[:, 0])[:, None], north[:, 1:]], axis=1)
    ext = jnp.concatenate([south, wide, north], axis=1)
    once = sweep(ext[:levels], ext[levels, 1:-1, 1:-1])
    return sweep(once, jnp.where(ocean, 0.0, coef))


def body(
    state,
    diffusion,
    exchange_rate,
    land_mask,
    fold_map,
    entry_tile,
    entry_source,
    entry_dest,
    entry_weight,
):
    field = state[0]
    levels, rows, cols = field.shape
    tiles = lax.axis_size("tx") * lax.axis_size("ty")
    entries = entry_source.shape[2]
    ocean = lax.axis_index("mp") == 1
    active = jnp.where(ocean, land_mask.astype(jnp.float32), 1.0)
    moved = mix(field, diffusion[0] * active, ocean, fold_map)

    sent = jnp.transpose(field.astype(jnp.bfloat16), (1, 0, 2))
    source, tile, dest = entry_source[0, 0], entry_tile[0, 0, :, 0], entry_dest[0, 0]
    count = entries // PARTS
    arrived = []
    for part in range(PARTS):
        pieces = contribute(part * count, count, sent, entry_weight[0, 0], source, tile, dest)
        pieces = pieces.reshape(tiles, count, LANES)
        arrived.append(
            lax.all_to_all(pieces, TILE_AXES, split_axis=0, concat_axis=0, tiled=True).reshape(-1, LANES)
        )
    summed = gather_rows(jnp.concatenate(arrived, axis=0), tiles, rows).reshape(tiles, rows, LANES)
    received = lax.all_to_all(summed, TILE_AXES, split_axis=0, concat_axis=0, tiled=True)
    received = lax.ppermute(received, "mp", [(0, 1), (1, 0)])
    result = finish(received, field, moved, exchange_rate[0] * active)
    return result[None]


def solution(mesh):
    in_specs = (
        P("mp", None, "tx", "ty"),
        P("mp", "tx", "ty"),
        P("mp", "tx", "ty"),
        P("tx", "ty"),
        P("ty"),
        P("mp", "tx", "ty", None),
        P("mp", "tx", "ty"),
        P("mp", "tx", "ty"),
        P("mp", "tx", "ty", None, None),
    )
    out_specs = P("mp", None, "tx", "ty")
    return jax.shard_map(body, mesh=mesh, in_specs=in_specs, out_specs=out_specs, check_vma=False)
```

```python
import functools

import jax
import jax.numpy as jnp
from jax import lax
from jax.experimental import pallas as pl
from jax.experimental.pallas import tpu as pltpu
from jax.sharding import PartitionSpec as P

TILE_AXES = ("tx", "ty")
QUARTERS = 4
LANES = 128
PACK = 16
WIDTH = 120
BLOCK = 40
ROW_BLOCK = 256
VMEM_LIMIT = 40 * 1024 * 1024


def spans(cols):
    return [(q * WIDTH, min(cols, (q + 1) * WIDTH)) for q in range(QUARTERS)]


def contribute_kernel(cols, source, tile, dest, state, weight, out, loose, picks, product, turned):
    levels, rows, _ = state.shape
    entries = weight.shape[1]
    step = pl.program_id(0)
    steps = WIDTH // BLOCK
    groups = entries // PACK
    lane = lax.broadcasted_iota(jnp.int32, (1, LANES), 1)

    @pl.when(step == 0)
    def prepare():
        place = lax.broadcasted_iota(jnp.int32, (entries, rows), 0)
        wanted = jnp.zeros((entries, rows), jnp.int32)
        for entry in range(entries):
            wanted = jnp.where(place == entry, source[entry], wanted)
        onehot = jnp.where(wanted == lax.broadcasted_iota(jnp.int32, (entries, rows), 1), 1.0, 0.0)
        onehot = onehot.astype(jnp.bfloat16)
        for level in range(levels):
            picked = jnp.dot(
                onehot, state[level].astype(jnp.bfloat16), preferred_element_type=jnp.float32
            )
            for half in range(2 * groups):
                loose[half, level * 8 : level * 8 + 8, :] = picked[half * 8 : half * 8 + 8]
        for group in range(groups):
            for half in range(2):
                picks[group, half * LANES : (half + 1) * LANES, :] = loose[2 * group + half].astype(
                    jnp.bfloat16
                )
        below = lax.broadcasted_iota(jnp.int32, (8, LANES), 0)
        for half in range(2 * groups):
            tiles = jnp.zeros((8, LANES), jnp.int32)
            dests = jnp.zeros((8, LANES), jnp.int32)
            for e in range(8):
                here = lax.broadcasted_iota(jnp.int32, (8, LANES), 1) % 8 == e
                tiles = jnp.where(here, tile[half * 8 + e], tiles)
                dests = jnp.where(here, dest[half * 8 + e], dests)
            tail = jnp.where(below == 6, tiles, jnp.where(below == 7, dests, 0))
            turned[WIDTH:LANES, half * LANES : (half + 1) * LANES] = tail.astype(jnp.float32)

    base = pl.multiple_of((step % steps) * BLOCK, 8)
    column = lax.broadcasted_iota(jnp.int32, (BLOCK, LANES), 0) + step * BLOCK
    for group in range(groups):
        streamed = weight[:, group * PACK : (group + 1) * PACK, :].reshape(BLOCK * PACK, cols)
        whole = lax.dot_general(
            streamed, picks[group], (((1,), (1,)), ((), ())), preferred_element_type=jnp.float32
        ).reshape(BLOCK, PACK, 2 * LANES)
        for half in range(2):
            slot = 2 * group + half
            own = whole[:, half * 8 : half * 8 + 8, half * LANES : (half + 1) * LANES]
            product[slot] = own.reshape(BLOCK * 8, LANES)
            y = jnp.zeros((BLOCK, LANES), jnp.float32)
            for e in range(8):
                y = jnp.where(lane % 8 == e, product[slot, pl.ds(e, BLOCK, stride=8), :], y)
            y = jnp.where(column < cols, y, 0.0)
            turned[pl.ds(base, BLOCK), slot * LANES : (slot + 1) * LANES] = y

    @pl.when(step % steps == steps - 1)
    def turn():
        quarter = step // steps
        for slot in range(2 * groups):
            block = turned[:, slot * LANES : (slot + 1) * LANES].T
            for level in range(levels):
                start = pl.multiple_of((level * QUARTERS + quarter) * entries + slot * 8, 8)
                out[pl.ds(start, 8), :] = block[level * 8 : level * 8 + 8]


def contribute(state, weight, source, tile, dest):
    levels, rows, cols = state.shape
    entries = weight.shape[1]
    groups = entries // PACK
    grid_spec = pltpu.PrefetchScalarGridSpec(
        num_scalar_prefetch=3,
        grid=(QUARTERS * WIDTH // BLOCK,),
        in_specs=[
            pl.BlockSpec((levels, rows, cols), lambda i, *_: (0, 0, 0)),
            pl.BlockSpec((BLOCK, entries, cols), lambda i, *_: (i, 0, 0)),
        ],
        out_specs=pl.BlockSpec((levels * QUARTERS * entries, LANES), lambda i, *_: (0, 0)),
        scratch_shapes=[
            pltpu.VMEM((2 * groups, LANES, cols), jnp.float32),
            pltpu.VMEM((groups, 2 * LANES, cols), jnp.bfloat16),
            pltpu.VMEM((2 * groups, BLOCK * 8, LANES), jnp.float32),
            pltpu.VMEM((LANES, 2 * groups * LANES), jnp.float32),
        ],
    )
    return pl.pallas_call(
        functools.partial(contribute_kernel, cols),
        grid_spec=grid_spec,
        out_shape=jax.ShapeDtypeStruct((levels * QUARTERS * entries, LANES), jnp.float32),
        compiler_params=pltpu.CompilerParams(vmem_limit_bytes=VMEM_LIMIT),
        cost_estimate=pl.CostEstimate(
            flops=2 * entries * levels * cols * cols,
            bytes_accessed=2 * entries * cols * cols,
            transcendentals=0,
        ),
        name="contribute",
    )(source, tile, dest, state, weight)


def gather_rows_kernel(tile_rows, values, out, halves, labels):
    block = pl.program_id(0)

    @pl.when(block == 0)
    def prepare():
        x = values[...]
        high = x.astype(jnp.bfloat16)
        low = (x - high.astype(jnp.float32)).astype(jnp.bfloat16)
        halves[:, :LANES] = high
        halves[:, LANES:] = low
        lane = lax.broadcasted_iota(jnp.int32, (8, LANES), 1)
        pick = jnp.where(lane == LANES - 2, float(tile_rows), jnp.where(lane == LANES - 1, 1.0, 0.0))
        labels[...] = lax.dot_general(
            pick.astype(jnp.bfloat16), high, (((1,), (1,)), ((), ())), preferred_element_type=jnp.float32
        ).astype(jnp.int32)

    count = values.shape[0]
    row = lax.broadcasted_iota(jnp.int32, (ROW_BLOCK, count), 0) + block * ROW_BLOCK
    onehot = jnp.where(row == labels[0:1, :], 1.0, 0.0).astype(jnp.bfloat16)
    sums = jnp.dot(onehot, halves[...], preferred_element_type=jnp.float32)
    out[...] = sums[:, :LANES] + sums[:, LANES:]


def gather_rows(values, tiles, tile_rows):
    count = values.shape[0]
    return pl.pallas_call(
        functools.partial(gather_rows_kernel, tile_rows),
        grid=(tiles * tile_rows // ROW_BLOCK,),
        in_specs=[pl.BlockSpec((count, LANES), lambda i: (0, 0))],
        out_specs=pl.BlockSpec((ROW_BLOCK, LANES), lambda i: (i, 0)),
        out_shape=jax.ShapeDtypeStruct((tiles * tile_rows, LANES), jnp.float32),
        scratch_shapes=[
            pltpu.VMEM((count, 2 * LANES), jnp.bfloat16),
            pltpu.VMEM((8, count), jnp.int32),
        ],
        compiler_params=pltpu.CompilerParams(vmem_limit_bytes=VMEM_LIMIT),
        name="gather_rows",
    )(values)


def finish_kernel(received, field, moved, rate, out):
    levels, rows, cols = field.shape
    for level in range(levels):
        parts = [
            received[level * QUARTERS + q][:, : high - low] for q, (low, high) in enumerate(spans(cols))
        ]
        whole = jnp.concatenate(parts, axis=1)
        out[level] = moved[level] + rate[...] * (whole - field[level])


def finish(received, field, moved, rate):
    return pl.pallas_call(
        finish_kernel,
        out_shape=jax.ShapeDtypeStruct(field.shape, jnp.float32),
        compiler_params=pltpu.CompilerParams(vmem_limit_bytes=VMEM_LIMIT),
        name="finish",
    )(received, field, moved, rate)


def shift(value, axis, forward, periodic):
    count = lax.axis_size(axis)
    pairs = [(i, i + 1) for i in range(count - 1)] + ([(count - 1, 0)] if periodic else [])
    if not forward:
        pairs = [(b, a) for a, b in pairs]
    return lax.ppermute(value, axis, pairs)


def sweep(f, c):
    mid = f[:, 1:-1, 1:-1]
    around = f[:, 2:, 1:-1] + f[:, :-2, 1:-1] + f[:, 1:-1, 2:] + f[:, 1:-1, :-2]
    return mid + c * (around - 4.0 * mid)


def mix(field, coef, ocean, fold_map):
    levels, rows, cols = field.shape
    stack = jnp.concatenate([field, coef[None]], axis=0)
    west = shift(stack[:, :, cols - 2 :], "ty", True, True)
    east = shift(stack[:, :, :2], "ty", False, True)
    wide = jnp.concatenate([west, stack, east], axis=2)
    south = shift(wide[:, rows - 2 :], "tx", True, False)
    north = shift(wide[:, :2], "tx", False, False)
    last = jnp.broadcast_to(field[None, :, rows - 1], (lax.axis_size("ty"), levels, cols))
    whole = lax.all_to_all(last, "ty", split_axis=0, concat_axis=0, tiled=True)
    whole = jnp.transpose(whole, (1, 0, 2)).reshape(levels, -1)
    folded = jnp.take(whole, fold_map, axis=1)
    fold_here = jnp.logical_and(ocean, lax.axis_index("tx") == lax.axis_size("tx") - 1)
    folded = jnp.pad(folded, ((0, 1), (2, 2)))
    north = jnp.concatenate([jnp.where(fold_here, folded, north[:, 0])[:, None], north[:, 1:]], axis=1)
    ext = jnp.concatenate([south, wide, north], axis=1)
    once = sweep(ext[:levels], ext[levels, 1:-1, 1:-1])
    return sweep(once, jnp.where(ocean, 0.0, coef))


def body(
    state,
    diffusion,
    exchange_rate,
    land_mask,
    fold_map,
    entry_tile,
    entry_source,
    entry_dest,
    entry_weight,
):
    field = state[0]
    levels, rows, cols = field.shape
    tiles = lax.axis_size("tx") * lax.axis_size("ty")
    entries = entry_source.shape[2]
    ocean = lax.axis_index("mp") == 1
    active = jnp.where(ocean, land_mask.astype(jnp.float32), 1.0)
    moved = mix(field, diffusion[0] * active, ocean, fold_map)

    source, tile, dest = entry_source[0, 0], entry_tile[0, 0, :, 0], entry_dest[0, 0]
    weight = jnp.transpose(entry_weight[0, 0], (1, 0, 2))
    pieces = contribute(field, weight, source, tile, dest).reshape(tiles, entries, LANES)
    arrived = lax.all_to_all(pieces, TILE_AXES, split_axis=0, concat_axis=0, tiled=True)
    arrived, moved = lax.optimization_barrier((arrived, moved))
    summed = gather_rows(arrived.reshape(-1, LANES), tiles, rows).reshape(tiles, rows, LANES)
    received = lax.all_to_all(summed, TILE_AXES, split_axis=0, concat_axis=0, tiled=True)
    received = lax.ppermute(received, "mp", [(0, 1), (1, 0)])
    result = finish(received, field, moved, exchange_rate[0] * active)
    return result[None]


def solution(mesh):
    in_specs = (
        P("mp", None, "tx", "ty"),
        P("mp", "tx", "ty"),
        P("mp", "tx", "ty"),
        P("tx", "ty"),
        P("ty"),
        P("mp", "tx", "ty", None),
        P("mp", "tx", "ty"),
        P("mp", "tx", "ty"),
        P("mp", "tx", "ty", None, None),
    )
    out_specs = P("mp", None, "tx", "ty")
    return jax.shard_map(body, mesh=mesh, in_specs=in_specs, out_specs=out_specs, check_vma=False)
```

```python
import functools

import jax
import jax.numpy as jnp
from jax import lax
from jax.experimental import pallas as pl
from jax.experimental.pallas import tpu as pltpu
from jax.sharding import PartitionSpec as P

TILE_AXES = ("tx", "ty")
QUARTERS = 4
LANES = 128
PACK = 16
WIDTH = 120
BLOCK = 30
FETCHES = (0, 30, 90, 150, 240, 330)
ROW_BLOCK = 1024
VMEM_LIMIT = 40 * 1024 * 1024


def spans(cols):
    return [(q * WIDTH, min(cols, (q + 1) * WIDTH)) for q in range(QUARTERS)]


def contribute_kernel(
    source, tile, dest, state, weight, out, field, blocks, loose, picks, product, turned, ready, sems, sent
):
    levels, rows, cols = state.shape
    entries = weight.shape[1]
    per_quarter = WIDTH // BLOCK
    groups = entries // PACK
    steps = -(-cols // BLOCK)
    lane = lax.broadcasted_iota(jnp.int32, (1, LANES), 1)

    fetch_state = pltpu.make_async_copy(state, field, sent.at[QUARTERS])
    fetch_state.start()
    fetches = {}
    for number, (low, high) in enumerate(zip(FETCHES, FETCHES[1:] + (cols,))):
        span = pl.ds(low, high - low)
        fetches[low] = pltpu.make_async_copy(weight.at[span], blocks.at[span], sems.at[number])
        fetches[low].start()

    place = lax.broadcasted_iota(jnp.int32, (entries, rows), 0)
    wanted = jnp.zeros((entries, rows), jnp.int32)
    for entry in range(entries):
        wanted = jnp.where(place == entry, source[entry], wanted)
    onehot = jnp.where(wanted == lax.broadcasted_iota(jnp.int32, (entries, rows), 1), 1.0, 0.0)
    onehot = onehot.astype(jnp.bfloat16)
    below = lax.broadcasted_iota(jnp.int32, (8, LANES), 0)
    here = lax.broadcasted_iota(jnp.int32, (8, LANES), 1) % 8
    for slot in range(2 * groups):
        tiles = jnp.zeros((8, LANES), jnp.int32)
        dests = jnp.zeros((8, LANES), jnp.int32)
        for e in range(8):
            tiles = jnp.where(here == e, tile[slot * 8 + e], tiles)
            dests = jnp.where(here == e, dest[slot * 8 + e], dests)
        tail = jnp.where(below == 6, tiles, jnp.where(below == 7, dests, 0))
        turned[WIDTH:LANES, slot * LANES : (slot + 1) * LANES] = tail.astype(jnp.float32)
    fetch_state.wait()
    for level in range(levels):
        picked = jnp.dot(onehot, field[level].astype(jnp.bfloat16), preferred_element_type=jnp.float32)
        for slot in range(2 * groups):
            loose[slot, level * 8 : level * 8 + 8, :] = picked[slot * 8 : slot * 8 + 8]
    for group in range(groups):
        for half in range(2):
            picks[group, half * LANES : (half + 1) * LANES, :] = loose[2 * group + half].astype(jnp.bfloat16)

    sends = []
    for step in range(steps):
        if step * BLOCK in fetches:
            fetches[step * BLOCK].wait()
        base = (step % per_quarter) * BLOCK
        for group in range(groups):
            streamed = blocks[step * BLOCK : (step + 1) * BLOCK, group * PACK : (group + 1) * PACK, :]
            whole = lax.dot_general(
                streamed.reshape(BLOCK * PACK, cols),
                picks[group],
                (((1,), (1,)), ((), ())),
                preferred_element_type=jnp.float32,
            ).reshape(BLOCK, PACK, 2 * LANES)
            for half in range(2):
                slot = 2 * group + half
                own = whole[:, half * 8 : half * 8 + 8, half * LANES : (half + 1) * LANES]
                product[slot] = own.reshape(BLOCK * 8, LANES)
                y = jnp.zeros((BLOCK, LANES), jnp.float32)
                for e in range(8):
                    y = jnp.where(lane % 8 == e, product[slot, pl.ds(e, BLOCK, stride=8), :], y)
                if (step + 1) * BLOCK > cols:
                    column = lax.broadcasted_iota(jnp.int32, (BLOCK, LANES), 0) + step * BLOCK
                    y = jnp.where(column < cols, y, 0.0)
                turned[base : base + BLOCK, slot * LANES : (slot + 1) * LANES] = y
        if step % per_quarter == per_quarter - 1 or step == steps - 1:
            quarter = step // per_quarter
            for slot in range(2 * groups):
                block = turned[:, slot * LANES : (slot + 1) * LANES].T
                for level in range(levels):
                    ready[quarter, level, slot * 8 : slot * 8 + 8, :] = block[level * 8 : level * 8 + 8]
            sends.append(pltpu.make_async_copy(ready.at[quarter], out.at[:, quarter], sent.at[quarter]))
            sends[-1].start()
    for send in sends:
        send.wait()


def contribute(state, weight, source, tile, dest):
    levels, rows, cols = state.shape
    entries = weight.shape[1]
    groups = entries // PACK
    steps = -(-cols // BLOCK)
    scalars = pl.BlockSpec(memory_space=pltpu.SMEM)
    away = pl.BlockSpec(memory_space=pltpu.HBM)
    return pl.pallas_call(
        contribute_kernel,
        in_specs=[scalars, scalars, scalars, away, away],
        out_specs=away,
        scratch_shapes=[
            pltpu.VMEM((levels, rows, cols), jnp.float32),
            pltpu.VMEM((steps * BLOCK, entries, cols), jnp.bfloat16),
            pltpu.VMEM((2 * groups, LANES, cols), jnp.float32),
            pltpu.VMEM((groups, 2 * LANES, cols), jnp.bfloat16),
            pltpu.VMEM((2 * groups, BLOCK * 8, LANES), jnp.float32),
            pltpu.VMEM((LANES, 2 * groups * LANES), jnp.float32),
            pltpu.VMEM((QUARTERS, levels, entries, LANES), jnp.float32),
            pltpu.SemaphoreType.DMA((len(FETCHES),)),
            pltpu.SemaphoreType.DMA((QUARTERS + 1,)),
        ],
        out_shape=jax.ShapeDtypeStruct((levels, QUARTERS, entries, LANES), jnp.float32),
        compiler_params=pltpu.CompilerParams(vmem_limit_bytes=VMEM_LIMIT),
        cost_estimate=pl.CostEstimate(
            flops=2 * entries * levels * cols * cols,
            bytes_accessed=2 * entries * cols * cols,
            transcendentals=0,
        ),
        name="contribute",
    )(source, tile, dest, state, weight)


def gather_rows_kernel(tile_rows, values, out, halves, labels):
    block = pl.program_id(0)

    @pl.when(block == 0)
    def prepare():
        x = values[...]
        high = x.astype(jnp.bfloat16)
        low = (x - high.astype(jnp.float32)).astype(jnp.bfloat16)
        halves[:, :LANES] = high
        halves[:, LANES:] = low
        lane = lax.broadcasted_iota(jnp.int32, (8, LANES), 1)
        pick = jnp.where(lane == LANES - 2, float(tile_rows), jnp.where(lane == LANES - 1, 1.0, 0.0))
        labels[...] = lax.dot_general(
            pick.astype(jnp.bfloat16), high, (((1,), (1,)), ((), ())), preferred_element_type=jnp.float32
        ).astype(jnp.int32)

    count = values.shape[0]
    row = lax.broadcasted_iota(jnp.int32, (ROW_BLOCK, count), 0) + block * ROW_BLOCK
    onehot = jnp.where(row == labels[0:1, :], 1.0, 0.0).astype(jnp.bfloat16)
    sums = jnp.dot(onehot, halves[...], preferred_element_type=jnp.float32)
    out[...] = sums[:, :LANES] + sums[:, LANES:]


def gather_rows(values, tiles, tile_rows):
    count = values.shape[0]
    return pl.pallas_call(
        functools.partial(gather_rows_kernel, tile_rows),
        grid=(tiles * tile_rows // ROW_BLOCK,),
        in_specs=[pl.BlockSpec((count, LANES), lambda i: (0, 0))],
        out_specs=pl.BlockSpec((ROW_BLOCK, LANES), lambda i: (i, 0)),
        out_shape=jax.ShapeDtypeStruct((tiles * tile_rows, LANES), jnp.float32),
        scratch_shapes=[
            pltpu.VMEM((count, 2 * LANES), jnp.bfloat16),
            pltpu.VMEM((8, count), jnp.int32),
        ],
        compiler_params=pltpu.CompilerParams(vmem_limit_bytes=VMEM_LIMIT),
        name="gather_rows",
    )(values)


def coefficient(flags, diffusion, mask):
    return diffusion * jnp.where(flags[0] == 1, mask.astype(jnp.float32), 1.0)


def edges_kernel(first, last, bottom, diffusion, low, high):
    levels, rows, _ = first.shape
    cols = diffusion.shape[1]
    end = (cols - 2) % LANES
    starts = [first[level][:, :2] for level in range(levels)] + [diffusion[:, :2]]
    ends = [last[level][:, end : end + 2] for level in range(levels)] + [diffusion[:, cols - 2 :]]
    edge = jnp.concatenate([bottom[level, 7:8, :] for level in range(levels)], axis=0)
    for out, pairs in ((low, starts), (high, ends)):
        message = jnp.concatenate(pairs, axis=1)
        out[:levels, :cols] = edge
        for part in range(rows // 8):
            start = part * LANES
            out[levels:, start : start + message.shape[1]] = message[part * 8 : part * 8 + 8]


def edges(field, diffusion):
    levels, rows, cols = field.shape
    out = jax.ShapeDtypeStruct((levels + 8, rows // 8 * LANES), jnp.float32)
    message = pl.BlockSpec(out.shape, lambda i: (0, 0))
    return pl.pallas_call(
        edges_kernel,
        grid=(1,),
        in_specs=[
            pl.BlockSpec((levels, rows, LANES), lambda i: (0, 0, 0)),
            pl.BlockSpec((levels, rows, LANES), lambda i: (0, 0, (cols - 2) // LANES)),
            pl.BlockSpec((levels, 8, cols), lambda i: (0, rows // 8 - 1, 0)),
            pl.BlockSpec((rows, cols), lambda i: (0, 0)),
        ],
        out_specs=[message, message],
        out_shape=[out, out],
        name="edges",
    )(field, field, field, diffusion)


def columns(message, rows):
    tall = message.shape[0]
    parts = [message[tall - 8 :, part * LANES : (part + 1) * LANES] for part in range(rows // 8)]
    return jnp.concatenate(parts, axis=0)


def rims_kernel(first, last, diffusion, west, east, low, high, three):
    levels, _, cols = first.shape
    rows = diffusion.shape[0]
    left, right = columns(west, rows), columns(east, rows)
    low[...] = jnp.zeros(low.shape, jnp.float32)
    high[...] = jnp.zeros(high.shape, jnp.float32)
    for out, block, start in ((low, first, 0), (high, last, rows - 2)):
        for level in range(levels + 1):
            place = pl.ds(2 * level, 2)
            if level < levels:
                out[place, LANES : LANES + cols] = block[level, start % 8 : start % 8 + 2, :]
            else:
                out[place, LANES : LANES + cols] = diffusion[start : start + 2, :]
            out[place, LANES - 2 : LANES] = left[start : start + 2, 2 * level : 2 * level + 2]
            out[place, LANES + cols : LANES + cols + 2] = right[start : start + 2, 2 * level : 2 * level + 2]
    three[0] = west[:levels, :cols]
    three[1] = jnp.concatenate([last[level, 7:8, :] for level in range(levels)], axis=0)
    three[2] = east[:levels, :cols]


def rims(field, diffusion, west, east):
    levels, rows, cols = field.shape
    wide = LANES * (2 + -(-cols // LANES))
    rim = jax.ShapeDtypeStruct((2 * levels + 2, wide), jnp.float32)
    three = jax.ShapeDtypeStruct((3, levels, cols), jnp.float32)
    whole = lambda shape: pl.BlockSpec(shape, lambda i: (0,) * len(shape))
    return pl.pallas_call(
        rims_kernel,
        grid=(1,),
        in_specs=[
            pl.BlockSpec((levels, 8, cols), lambda i: (0, 0, 0)),
            pl.BlockSpec((levels, 8, cols), lambda i: (0, rows // 8 - 1, 0)),
            whole((rows, cols)),
            whole(west.shape),
            whole(east.shape),
        ],
        out_specs=[whole(rim.shape), whole(rim.shape), whole(three.shape)],
        out_shape=[rim, rim, three],
        name="rims",
    )(field, field, diffusion, west, east)


def mix_kernel(
    flags, field, diffusion, rate, mask, west, east, south, north, near, behind, ahead, fold_map, out, ext, coefs, folded, sides
):
    part, rows, cols = field.shape
    levels = near.shape[1]
    step = pl.program_id(0)
    own_rows, own_lanes = slice(8, 8 + rows), slice(LANES, LANES + cols)
    active = coefficient(flags, 1.0, mask[...])

    @pl.when(step == 0)
    def prepare():
        ext[...] = jnp.zeros(ext.shape, jnp.float32)
        coefs[...] = jnp.zeros(coefs.shape, jnp.float32)
        coefs[own_rows, own_lanes] = diffusion[...] * active
        sides[0] = columns(west, rows)
        sides[1] = columns(east, rows)
        coefs[own_rows, LANES - 2 : LANES] = sides[0, :, 2 * levels : 2 * levels + 2]
        coefs[own_rows, LANES + cols : LANES + cols + 2] = sides[1, :, 2 * levels : 2 * levels + 2]
        coefs[6:8, :] = south[2 * levels : 2 * levels + 2, :]
        coefs[8 + rows : 10 + rows, :] = north[2 * levels : 2 * levels + 2, :]

    @pl.when(jnp.logical_and(step == 0, flags[1] == 1))
    def fold():
        total = jnp.zeros((3 * levels, cols), jnp.float32)
        place = lax.broadcasted_iota(jnp.int32, (cols, cols), 0)
        held = [behind[1], behind[2], near[0], near[1], near[2], ahead[0], ahead[1], ahead[2]]
        for number, whole in enumerate(held):
            copy = (flags[2] + number + 5) % 8
            high = whole.astype(jnp.bfloat16).astype(jnp.float32)
            rest = whole - high
            middle = rest.astype(jnp.bfloat16).astype(jnp.float32)
            parts = jnp.concatenate([high, middle, rest - middle], axis=0).astype(jnp.bfloat16)
            onehot = jnp.where(place + copy * cols == fold_map[...], 1.0, 0.0).astype(jnp.bfloat16)
            total = total + jnp.dot(parts, onehot, preferred_element_type=jnp.float32)
        folded[...] = total[:levels] + total[levels : 2 * levels] + total[2 * levels :]

    tall, wide = ext.shape[1:]
    again = jnp.where(flags[0] == 1, 0.0, 1.0)

    def sweep(f, c):
        around = pltpu.roll(f, 1, 0) + pltpu.roll(f, tall - 1, 0)
        around = around + pltpu.roll(f, 1, 1) + pltpu.roll(f, wide - 1, 1)
        return f + c * (around - 4.0 * f)

    for local in range(part):
        ext[local, own_rows, own_lanes] = field[local]

    for number in range(levels // part):

        @pl.when(step == number)
        def outside():
            for local in range(part):
                level = number * part + local
                pair = slice(2 * level, 2 * level + 2)
                ext[local, own_rows, LANES - 2 : LANES] = sides[0, :, pair]
                ext[local, own_rows, LANES + cols : LANES + cols + 2] = sides[1, :, pair]
                ext[local, 6:8, :] = south[pair, :]
                ext[local, 8 + rows : 10 + rows, :] = north[pair, :]

        @pl.when(jnp.logical_and(step == number, flags[1] == 1))
        def folded_rows():
            for local in range(part):
                level = number * part + local
                ext[local, 8 + rows : 9 + rows, own_lanes] = folded[level : level + 1, :]

    for local in range(part):
        once = sweep(ext[local], coefs[...])
        twice = sweep(once, coefs[...] * again)
        out[local] = twice[own_rows, own_lanes] - rate[...] * active * field[local]


def mix(flags, field, diffusion, rate, mask, west, east, south, north, near, behind, ahead, fold_map):
    levels, rows, cols = field.shape
    part = 4
    wide = south.shape[1]
    whole = lambda shape: pl.BlockSpec(shape, lambda i: (0,) * len(shape))
    block = pl.BlockSpec((part, rows, cols), lambda i: (i, 0, 0))
    return pl.pallas_call(
        mix_kernel,
        grid=(levels // part,),
        in_specs=[
            pl.BlockSpec(memory_space=pltpu.SMEM),
            block,
            whole((rows, cols)),
            whole((rows, cols)),
            whole((rows, cols)),
            whole(west.shape),
            whole(east.shape),
            whole(south.shape),
            whole(north.shape),
            whole(near.shape),
            whole(behind.shape),
            whole(ahead.shape),
            whole((1, cols)),
        ],
        out_specs=block,
        scratch_shapes=[
            pltpu.VMEM((part, rows + 16, wide), jnp.float32),
            pltpu.VMEM((rows + 16, wide), jnp.float32),
            pltpu.VMEM((levels, cols), jnp.float32),
            pltpu.VMEM((2, rows, LANES), jnp.float32),
        ],
        out_shape=jax.ShapeDtypeStruct(field.shape, jnp.float32),
        name="mix",
    )(flags, field, diffusion, rate, mask, west, east, south, north, near, behind, ahead, fold_map[None])


def finish_kernel(flags, received, base, rate, mask, out, inner, outer, fetched, stored):
    levels, rows, cols = base.shape
    parts = fetched.shape[0]
    part = levels // parts
    fetches = []
    for number in range(parts):
        span = pl.ds(number * part, part)
        fetches.append(pltpu.make_async_copy(base.at[span], inner.at[span], fetched.at[number]))
        fetches[-1].start()
    pull = coefficient(flags, rate[...], mask[...])
    stores = []
    for number in range(parts):
        fetches[number].wait()
        for level in range(number * part, (number + 1) * part):
            pieces = [received[level * QUARTERS + q][:, : high - low] for q, (low, high) in enumerate(spans(cols))]
            outer[level] = inner[level] + pull * jnp.concatenate(pieces, axis=1)
        span = pl.ds(number * part, part)
        stores.append(pltpu.make_async_copy(outer.at[span], out.at[span], stored.at[number]))
        stores[-1].start()
    for store in stores:
        store.wait()


def finish(flags, received, base, rate, mask):
    parts = 4
    inside = pl.BlockSpec(memory_space=pltpu.VMEM)
    away = pl.BlockSpec(memory_space=pltpu.HBM)
    return pl.pallas_call(
        finish_kernel,
        in_specs=[pl.BlockSpec(memory_space=pltpu.SMEM), inside, away, inside, inside],
        out_specs=away,
        out_shape=jax.ShapeDtypeStruct(base.shape, jnp.float32),
        scratch_shapes=[
            pltpu.VMEM(base.shape, jnp.float32),
            pltpu.VMEM(base.shape, jnp.float32),
            pltpu.SemaphoreType.DMA((parts,)),
            pltpu.SemaphoreType.DMA((parts,)),
        ],
        compiler_params=pltpu.CompilerParams(vmem_limit_bytes=VMEM_LIMIT),
        name="finish",
    )(flags, received, base, rate, mask)


def shift(value, axis, forward, periodic):
    count = lax.axis_size(axis)
    pairs = [(i, i + 1) for i in range(count - 1)] + ([(count - 1, 0)] if periodic else [])
    if not forward:
        pairs = [(b, a) for a, b in pairs]
    return lax.ppermute(value, axis, pairs)


def across(value, distance):
    count = lax.axis_size("ty")
    start = 2 * lax.axis_size("tx") * count - count
    pairs = [(start + i, start + (i + distance) % count) for i in range(count)]
    return lax.ppermute(value, ("mp", "tx", "ty"), pairs)


def spread(value, axes):
    return lax.all_to_all(value, axes, split_axis=0, concat_axis=0, tiled=True)


def body(
    state,
    diffusion,
    exchange_rate,
    land_mask,
    fold_map,
    entry_tile,
    entry_source,
    entry_dest,
    entry_weight,
):
    field = state[0]
    levels, rows, cols = field.shape
    tiles = lax.axis_size("tx") * lax.axis_size("ty")
    entries = entry_source.shape[2]
    ocean = lax.axis_index("mp") == 1
    fold_here = jnp.logical_and(ocean, lax.axis_index("tx") == lax.axis_size("tx") - 1)
    flags = jnp.stack([ocean, fold_here, lax.axis_index("ty")]).astype(jnp.int32)
    low, high = edges(field, diffusion[0])
    west = shift(high, "ty", True, True)
    east = shift(low, "ty", False, True)

    source, tile, dest = entry_source[0, 0], entry_tile[0, 0, :, 0], entry_dest[0, 0]
    weight = jnp.transpose(entry_weight[0, 0], (1, 0, 2))
    pieces = contribute(field, weight, source, tile, dest)
    pieces, west, east = lax.optimization_barrier((pieces, west, east))
    arrived = spread(pieces.reshape(tiles, entries, LANES), TILE_AXES)

    low, high, near = rims(field, diffusion[0], west, east)
    south = shift(high, "tx", True, False)
    north = shift(low, "tx", False, False)
    behind = across(near, 3)
    ahead = across(near, -3)
    summed = gather_rows(arrived.reshape(-1, LANES), tiles, rows).reshape(tiles, rows, LANES)
    summed, south, north, behind, ahead = lax.optimization_barrier((summed, south, north, behind, ahead))
    base = mix(
        flags,
        field,
        diffusion[0],
        exchange_rate[0],
        land_mask,
        west,
        east,
        south,
        north,
        near,
        behind,
        ahead,
        fold_map,
    )
    received, base = lax.optimization_barrier((spread(summed, TILE_AXES), base))
    received = lax.ppermute(received, "mp", [(0, 1), (1, 0)])
    return finish(flags, received, base, exchange_rate[0], land_mask)[None]


def solution(mesh):
    in_specs = (
        P("mp", None, "tx", "ty"),
        P("mp", "tx", "ty"),
        P("mp", "tx", "ty"),
        P("tx", "ty"),
        P("ty"),
        P("mp", "tx", "ty", None),
        P("mp", "tx", "ty"),
        P("mp", "tx", "ty"),
        P("mp", "tx", "ty", None, None),
    )
    out_specs = P("mp", None, "tx", "ty")
    return jax.shard_map(body, mesh=mesh, in_specs=in_specs, out_specs=out_specs, check_vma=False)
```

```python
import functools

import jax
import jax.numpy as jnp
from jax import lax
from jax.experimental import pallas as pl
from jax.experimental.pallas import tpu as pltpu
from jax.sharding import PartitionSpec as P

TILE_AXES = ("tx", "ty")
QUARTERS = 4
LANES = 128
PACK = 16
WIDTH = 120
BLOCK = 30
FETCHES = (0, 30, 90, 150, 240, 330)
ROW_BLOCK = 1024
VMEM_LIMIT = 40 * 1024 * 1024
SMALL_LIMIT = 16 * 1024 * 1024
FULL_LIMIT = 60 * 1024 * 1024


def spans(cols):
    return [(q * WIDTH, min(cols, (q + 1) * WIDTH)) for q in range(QUARTERS)]


def contribute_kernel(
    source, tile, dest, state, weight, out, blocks, loose, picks, product, turned, ready, sems, sent
):
    levels, rows, cols = state.shape
    entries = weight.shape[1]
    per_quarter = WIDTH // BLOCK
    groups = entries // PACK
    steps = -(-cols // BLOCK)
    lane = lax.broadcasted_iota(jnp.int32, (1, LANES), 1)

    fetches = {}
    for number, (low, high) in enumerate(zip(FETCHES, FETCHES[1:] + (cols,))):
        span = pl.ds(low, high - low)
        fetches[low] = pltpu.make_async_copy(weight.at[span], blocks.at[span], sems.at[number])
        fetches[low].start()

    place = lax.broadcasted_iota(jnp.int32, (entries, rows), 0)
    wanted = jnp.zeros((entries, rows), jnp.int32)
    for entry in range(entries):
        wanted = jnp.where(place == entry, source[entry], wanted)
    onehot = jnp.where(wanted == lax.broadcasted_iota(jnp.int32, (entries, rows), 1), 1.0, 0.0)
    onehot = onehot.astype(jnp.bfloat16)
    below = lax.broadcasted_iota(jnp.int32, (8, LANES), 0)
    here = lax.broadcasted_iota(jnp.int32, (8, LANES), 1) % 8
    for slot in range(2 * groups):
        tiles = jnp.zeros((8, LANES), jnp.int32)
        dests = jnp.zeros((8, LANES), jnp.int32)
        for e in range(8):
            tiles = jnp.where(here == e, tile[slot * 8 + e], tiles)
            dests = jnp.where(here == e, dest[slot * 8 + e], dests)
        tail = jnp.where(below == 6, tiles, jnp.where(below == 7, dests, 0))
        turned[WIDTH:LANES, slot * LANES : (slot + 1) * LANES] = tail.astype(jnp.float32)
    for level in range(levels):
        picked = jnp.dot(onehot, state[level].astype(jnp.bfloat16), preferred_element_type=jnp.float32)
        for slot in range(2 * groups):
            loose[slot, level * 8 : level * 8 + 8, :] = picked[slot * 8 : slot * 8 + 8]
    for group in range(groups):
        for half in range(2):
            picks[group, half * LANES : (half + 1) * LANES, :] = loose[2 * group + half].astype(jnp.bfloat16)

    sends = []
    for step in range(steps):
        if step * BLOCK in fetches:
            fetches[step * BLOCK].wait()
        base = (step % per_quarter) * BLOCK
        for group in range(groups):
            streamed = blocks[step * BLOCK : (step + 1) * BLOCK, group * PACK : (group + 1) * PACK, :]
            whole = lax.dot_general(
                streamed.reshape(BLOCK * PACK, cols),
                picks[group],
                (((1,), (1,)), ((), ())),
                preferred_element_type=jnp.float32,
            ).reshape(BLOCK, PACK, 2 * LANES)
            for half in range(2):
                slot = 2 * group + half
                own = whole[:, half * 8 : half * 8 + 8, half * LANES : (half + 1) * LANES]
                product[slot] = own.reshape(BLOCK * 8, LANES)
                y = jnp.zeros((BLOCK, LANES), jnp.float32)
                for e in range(8):
                    y = jnp.where(lane % 8 == e, product[slot, pl.ds(e, BLOCK, stride=8), :], y)
                if (step + 1) * BLOCK > cols:
                    column = lax.broadcasted_iota(jnp.int32, (BLOCK, LANES), 0) + step * BLOCK
                    y = jnp.where(column < cols, y, 0.0)
                turned[base : base + BLOCK, slot * LANES : (slot + 1) * LANES] = y
        if step % per_quarter == per_quarter - 1 or step == steps - 1:
            quarter = step // per_quarter
            for slot in range(2 * groups):
                block = turned[:, slot * LANES : (slot + 1) * LANES].T
                for level in range(levels):
                    ready[quarter, level, slot * 8 : slot * 8 + 8, :] = block[level * 8 : level * 8 + 8]
            sends.append(pltpu.make_async_copy(ready.at[quarter], out.at[:, quarter], sent.at[quarter]))
            sends[-1].start()
    for send in sends:
        send.wait()


def contribute(state, weight, source, tile, dest):
    levels, rows, cols = state.shape
    entries = weight.shape[1]
    groups = entries // PACK
    steps = -(-cols // BLOCK)
    scalars = pl.BlockSpec(memory_space=pltpu.SMEM)
    away = pl.BlockSpec(memory_space=pltpu.HBM)
    return pl.pallas_call(
        contribute_kernel,
        in_specs=[scalars, scalars, scalars, pl.BlockSpec(memory_space=pltpu.VMEM), away],
        out_specs=away,
        scratch_shapes=[
            pltpu.VMEM((steps * BLOCK, entries, cols), jnp.bfloat16),
            pltpu.VMEM((2 * groups, LANES, cols), jnp.float32),
            pltpu.VMEM((groups, 2 * LANES, cols), jnp.bfloat16),
            pltpu.VMEM((2 * groups, BLOCK * 8, LANES), jnp.float32),
            pltpu.VMEM((LANES, 2 * groups * LANES), jnp.float32),
            pltpu.VMEM((QUARTERS, levels, entries, LANES), jnp.float32),
            pltpu.SemaphoreType.DMA((len(FETCHES),)),
            pltpu.SemaphoreType.DMA((QUARTERS,)),
        ],
        out_shape=jax.ShapeDtypeStruct((levels, QUARTERS, entries, LANES), jnp.float32),
        compiler_params=pltpu.CompilerParams(vmem_limit_bytes=VMEM_LIMIT),
        cost_estimate=pl.CostEstimate(
            flops=2 * entries * levels * cols * cols,
            bytes_accessed=2 * entries * cols * cols,
            transcendentals=0,
        ),
        name="contribute",
    )(source, tile, dest, state, weight)


def gather_rows_kernel(tile_rows, values, out, halves, labels):
    block = pl.program_id(0)

    @pl.when(block == 0)
    def prepare():
        x = values[...]
        high = x.astype(jnp.bfloat16)
        low = (x - high.astype(jnp.float32)).astype(jnp.bfloat16)
        halves[:, :LANES] = high
        halves[:, LANES:] = low
        lane = lax.broadcasted_iota(jnp.int32, (8, LANES), 1)
        pick = jnp.where(lane == LANES - 2, float(tile_rows), jnp.where(lane == LANES - 1, 1.0, 0.0))
        labels[...] = lax.dot_general(
            pick.astype(jnp.bfloat16), high, (((1,), (1,)), ((), ())), preferred_element_type=jnp.float32
        ).astype(jnp.int32)

    count = values.shape[0]
    row = lax.broadcasted_iota(jnp.int32, (ROW_BLOCK, count), 0) + block * ROW_BLOCK
    onehot = jnp.where(row == labels[0:1, :], 1.0, 0.0).astype(jnp.bfloat16)
    sums = jnp.dot(onehot, halves[...], preferred_element_type=jnp.float32)
    out[...] = sums[:, :LANES] + sums[:, LANES:]


def gather_rows(values, tiles, tile_rows):
    count = values.shape[0]
    return pl.pallas_call(
        functools.partial(gather_rows_kernel, tile_rows),
        grid=(tiles * tile_rows // ROW_BLOCK,),
        in_specs=[pl.BlockSpec(memory_space=pltpu.VMEM)],
        out_specs=pl.BlockSpec((ROW_BLOCK, LANES), lambda i: (i, 0)),
        out_shape=jax.ShapeDtypeStruct((tiles * tile_rows, LANES), jnp.float32),
        scratch_shapes=[
            pltpu.VMEM((count, 2 * LANES), jnp.bfloat16),
            pltpu.VMEM((8, count), jnp.int32),
        ],
        compiler_params=pltpu.CompilerParams(vmem_limit_bytes=VMEM_LIMIT),
        name="gather_rows",
    )(values)


def coefficient(flags, diffusion, mask):
    return diffusion * jnp.where(flags[0] == 1, mask.astype(jnp.float32), 1.0)


def edges_kernel(first, last, bottom, diffusion, low, high):
    levels, rows, _ = first.shape
    cols = diffusion.shape[1]
    end = (cols - 2) % LANES
    starts = [first[level][:, :2] for level in range(levels)] + [diffusion[:, :2]]
    ends = [last[level][:, end : end + 2] for level in range(levels)] + [diffusion[:, cols - 2 :]]
    edge = jnp.concatenate([bottom[level, 7:8, :] for level in range(levels)], axis=0)
    for out, pairs in ((low, starts), (high, ends)):
        message = jnp.concatenate(pairs, axis=1)
        out[:levels, :cols] = edge
        for part in range(rows // 8):
            start = part * LANES
            out[levels:, start : start + message.shape[1]] = message[part * 8 : part * 8 + 8]


def edges(field, diffusion):
    levels, rows, cols = field.shape
    out = jax.ShapeDtypeStruct((levels + 8, rows // 8 * LANES), jnp.float32)
    message = pl.BlockSpec(out.shape, lambda i: (0, 0))
    return pl.pallas_call(
        edges_kernel,
        grid=(1,),
        in_specs=[
            pl.BlockSpec((levels, rows, LANES), lambda i: (0, 0, 0)),
            pl.BlockSpec((levels, rows, LANES), lambda i: (0, 0, (cols - 2) // LANES)),
            pl.BlockSpec((levels, 8, cols), lambda i: (0, rows // 8 - 1, 0)),
            pl.BlockSpec((rows, cols), lambda i: (0, 0)),
        ],
        out_specs=[message, message],
        out_shape=[out, out],
        compiler_params=pltpu.CompilerParams(vmem_limit_bytes=FULL_LIMIT),
        name="edges",
    )(field, field, field, diffusion)


def columns(message, rows):
    tall = message.shape[0]
    parts = [message[tall - 8 :, part * LANES : (part + 1) * LANES] for part in range(rows // 8)]
    return jnp.concatenate(parts, axis=0)


def rims_kernel(first, last, diffusion, west, east, low, high, three, sides):
    levels, _, cols = first.shape
    rows = diffusion.shape[0]
    left, right = columns(west, rows), columns(east, rows)
    sides[0] = left
    sides[1] = right
    low[...] = jnp.zeros(low.shape, jnp.float32)
    high[...] = jnp.zeros(high.shape, jnp.float32)
    for out, block, start in ((low, first, 0), (high, last, rows - 2)):
        for level in range(levels + 1):
            place = pl.ds(2 * level, 2)
            if level < levels:
                out[place, LANES : LANES + cols] = block[level, start % 8 : start % 8 + 2, :]
            else:
                out[place, LANES : LANES + cols] = diffusion[start : start + 2, :]
            out[place, LANES - 2 : LANES] = left[start : start + 2, 2 * level : 2 * level + 2]
            out[place, LANES + cols : LANES + cols + 2] = right[start : start + 2, 2 * level : 2 * level + 2]
    three[0] = west[:levels, :cols]
    three[1] = jnp.concatenate([last[level, 7:8, :] for level in range(levels)], axis=0)
    three[2] = east[:levels, :cols]


def rims(field, diffusion, west, east):
    levels, rows, cols = field.shape
    wide = LANES * (2 + -(-cols // LANES))
    rim = jax.ShapeDtypeStruct((2 * levels + 2, wide), jnp.float32)
    three = jax.ShapeDtypeStruct((3, levels, cols), jnp.float32)
    sides = jax.ShapeDtypeStruct((2, rows, LANES), jnp.float32)
    whole = lambda shape: pl.BlockSpec(shape, lambda i: (0,) * len(shape))
    return pl.pallas_call(
        rims_kernel,
        grid=(1,),
        in_specs=[
            pl.BlockSpec((levels, 8, cols), lambda i: (0, 0, 0)),
            pl.BlockSpec((levels, 8, cols), lambda i: (0, rows // 8 - 1, 0)),
            whole((rows, cols)),
            whole(west.shape),
            whole(east.shape),
        ],
        out_specs=[whole(rim.shape), whole(rim.shape), whole(three.shape), whole(sides.shape)],
        out_shape=[rim, rim, three, sides],
        compiler_params=pltpu.CompilerParams(vmem_limit_bytes=FULL_LIMIT),
        name="rims",
    )(field, field, diffusion, west, east)


def mix_kernel(
    flags, field, diffusion, rate, mask, sides, south, north, near, behind, ahead, fold_map, out, ext, coefs, folded
):
    part, rows, cols = field.shape
    levels = near.shape[1]
    step = pl.program_id(0)
    own_rows, own_lanes = slice(8, 8 + rows), slice(LANES, LANES + cols)
    active = coefficient(flags, 1.0, mask[...])

    @pl.when(step == 0)
    def prepare():
        ext[...] = jnp.zeros(ext.shape, jnp.float32)
        coefs[...] = jnp.zeros(coefs.shape, jnp.float32)
        coefs[own_rows, own_lanes] = diffusion[...] * active
        coefs[own_rows, LANES - 2 : LANES] = sides[0, :, 2 * levels : 2 * levels + 2]
        coefs[own_rows, LANES + cols : LANES + cols + 2] = sides[1, :, 2 * levels : 2 * levels + 2]
        coefs[6:8, :] = south[2 * levels : 2 * levels + 2, :]
        coefs[8 + rows : 10 + rows, :] = north[2 * levels : 2 * levels + 2, :]

    @pl.when(jnp.logical_and(step == 0, flags[1] == 1))
    def fold():
        total = jnp.zeros((3 * levels, cols), jnp.float32)
        place = lax.broadcasted_iota(jnp.int32, (cols, cols), 0)
        held = [behind[1], behind[2], near[0], near[1], near[2], ahead[0], ahead[1], ahead[2]]
        for number, whole in enumerate(held):
            copy = (flags[2] + number + 5) % 8
            high = whole.astype(jnp.bfloat16).astype(jnp.float32)
            rest = whole - high
            middle = rest.astype(jnp.bfloat16).astype(jnp.float32)
            parts = jnp.concatenate([high, middle, rest - middle], axis=0).astype(jnp.bfloat16)
            onehot = jnp.where(place + copy * cols == fold_map[...], 1.0, 0.0).astype(jnp.bfloat16)
            total = total + jnp.dot(parts, onehot, preferred_element_type=jnp.float32)
        folded[...] = total[:levels] + total[levels : 2 * levels] + total[2 * levels :]

    tall, wide = ext.shape[1:]
    again = jnp.where(flags[0] == 1, 0.0, 1.0)

    def sweep(f, c):
        around = pltpu.roll(f, 1, 0) + pltpu.roll(f, tall - 1, 0)
        around = around + pltpu.roll(f, 1, 1) + pltpu.roll(f, wide - 1, 1)
        return f + c * (around - 4.0 * f)

    for local in range(part):
        ext[local, own_rows, own_lanes] = field[local]

    for number in range(levels // part):

        @pl.when(step == number)
        def outside():
            for local in range(part):
                level = number * part + local
                pair = slice(2 * level, 2 * level + 2)
                ext[local, own_rows, LANES - 2 : LANES] = sides[0, :, pair]
                ext[local, own_rows, LANES + cols : LANES + cols + 2] = sides[1, :, pair]
                ext[local, 6:8, :] = south[pair, :]
                ext[local, 8 + rows : 10 + rows, :] = north[pair, :]

        @pl.when(jnp.logical_and(step == number, flags[1] == 1))
        def folded_rows():
            for local in range(part):
                level = number * part + local
                ext[local, 8 + rows : 9 + rows, own_lanes] = folded[level : level + 1, :]

    for local in range(part):
        once = sweep(ext[local], coefs[...])
        twice = sweep(once, coefs[...] * again)
        out[local] = twice[own_rows, own_lanes] - rate[...] * active * field[local]


def mix(flags, field, diffusion, rate, mask, sides, south, north, near, behind, ahead, fold_map):
    levels, rows, cols = field.shape
    part = 4
    wide = south.shape[1]
    whole = lambda shape: pl.BlockSpec(shape, lambda i: (0,) * len(shape))
    block = pl.BlockSpec((part, rows, cols), lambda i: (i, 0, 0))
    return pl.pallas_call(
        mix_kernel,
        grid=(levels // part,),
        in_specs=[
            pl.BlockSpec(memory_space=pltpu.SMEM),
            block,
            whole((rows, cols)),
            whole((rows, cols)),
            whole((rows, cols)),
            whole(sides.shape),
            whole(south.shape),
            whole(north.shape),
            whole(near.shape),
            whole(behind.shape),
            whole(ahead.shape),
            whole((1, cols)),
        ],
        out_specs=block,
        scratch_shapes=[
            pltpu.VMEM((part, rows + 16, wide), jnp.float32),
            pltpu.VMEM((rows + 16, wide), jnp.float32),
            pltpu.VMEM((levels, cols), jnp.float32),
        ],
        out_shape=jax.ShapeDtypeStruct(field.shape, jnp.float32),
        compiler_params=pltpu.CompilerParams(vmem_limit_bytes=SMALL_LIMIT),
        name="mix",
    )(flags, field, diffusion, rate, mask, sides, south, north, near, behind, ahead, fold_map[None])


def finish_kernel(flags, received, base, rate, mask, out, outer, stored):
    levels, rows, cols = base.shape
    parts = stored.shape[0]
    part = levels // parts
    pull = coefficient(flags, rate[...], mask[...])
    stores = []
    for number in range(parts):
        for level in range(number * part, (number + 1) * part):
            pieces = [received[level * QUARTERS + q][:, : high - low] for q, (low, high) in enumerate(spans(cols))]
            outer[level] = base[level] + pull * jnp.concatenate(pieces, axis=1)
        span = pl.ds(number * part, part)
        stores.append(pltpu.make_async_copy(outer.at[span], out.at[span], stored.at[number]))
        stores[-1].start()
    for store in stores:
        store.wait()


def finish(flags, received, base, rate, mask):
    parts = 4
    inside = pl.BlockSpec(memory_space=pltpu.VMEM)
    return pl.pallas_call(
        finish_kernel,
        in_specs=[pl.BlockSpec(memory_space=pltpu.SMEM), inside, inside, inside, inside],
        out_specs=pl.BlockSpec(memory_space=pltpu.HBM),
        out_shape=jax.ShapeDtypeStruct(base.shape, jnp.float32),
        scratch_shapes=[pltpu.VMEM(base.shape, jnp.float32), pltpu.SemaphoreType.DMA((parts,))],
        compiler_params=pltpu.CompilerParams(vmem_limit_bytes=SMALL_LIMIT),
        name="finish",
    )(flags, received, base, rate, mask)


def shift(value, axis, forward, periodic):
    count = lax.axis_size(axis)
    pairs = [(i, i + 1) for i in range(count - 1)] + ([(count - 1, 0)] if periodic else [])
    if not forward:
        pairs = [(b, a) for a, b in pairs]
    return lax.ppermute(value, axis, pairs)


def across(value, distance):
    count = lax.axis_size("ty")
    start = 2 * lax.axis_size("tx") * count - count
    pairs = [(start + i, start + (i + distance) % count) for i in range(count)]
    return lax.ppermute(value, ("mp", "tx", "ty"), pairs)


def spread(value, axes):
    return lax.all_to_all(value, axes, split_axis=0, concat_axis=0, tiled=True)


def body(
    state,
    diffusion,
    exchange_rate,
    land_mask,
    fold_map,
    entry_tile,
    entry_source,
    entry_dest,
    entry_weight,
):
    field = state[0]
    levels, rows, cols = field.shape
    tiles = lax.axis_size("tx") * lax.axis_size("ty")
    entries = entry_source.shape[2]
    ocean = lax.axis_index("mp") == 1
    fold_here = jnp.logical_and(ocean, lax.axis_index("tx") == lax.axis_size("tx") - 1)
    flags = jnp.stack([ocean, fold_here, lax.axis_index("ty")]).astype(jnp.int32)
    low, high = edges(field, diffusion[0])
    west = shift(high, "ty", True, True)
    east = shift(low, "ty", False, True)

    source, tile, dest = entry_source[0, 0], entry_tile[0, 0, :, 0], entry_dest[0, 0]
    weight = jnp.transpose(entry_weight[0, 0], (1, 0, 2))
    pieces = contribute(field, weight, source, tile, dest)
    pieces, west, east = lax.optimization_barrier((pieces, west, east))
    arrived = spread(pieces.reshape(tiles, entries, LANES), TILE_AXES)

    low, high, near, sides = rims(field, diffusion[0], west, east)
    south = shift(high, "tx", True, False)
    north = shift(low, "tx", False, False)
    behind = across(near, 3)
    ahead = across(near, -3)
    summed = gather_rows(arrived.reshape(-1, LANES), tiles, rows).reshape(tiles, rows, LANES)
    summed, south, north, behind, ahead = lax.optimization_barrier((summed, south, north, behind, ahead))
    base = mix(
        flags,
        field,
        diffusion[0],
        exchange_rate[0],
        land_mask,
        sides,
        south,
        north,
        near,
        behind,
        ahead,
        fold_map,
    )
    received, base = lax.optimization_barrier((spread(summed, TILE_AXES), base))
    received = lax.ppermute(received, "mp", [(0, 1), (1, 0)])
    return finish(flags, received, base, exchange_rate[0], land_mask)[None]


def solution(mesh):
    in_specs = (
        P("mp", None, "tx", "ty"),
        P("mp", "tx", "ty"),
        P("mp", "tx", "ty"),
        P("tx", "ty"),
        P("ty"),
        P("mp", "tx", "ty", None),
        P("mp", "tx", "ty"),
        P("mp", "tx", "ty"),
        P("mp", "tx", "ty", None, None),
    )
    out_specs = P("mp", None, "tx", "ty")
    return jax.shard_map(body, mesh=mesh, in_specs=in_specs, out_specs=out_specs, check_vma=False)
```

```python
import functools

import jax
import jax.numpy as jnp
from jax import lax
from jax.experimental import pallas as pl
from jax.experimental.pallas import tpu as pltpu
from jax.sharding import PartitionSpec as P

TILE_AXES = ("tx", "ty")
QUARTERS = 4
LANES = 128
SIDE = 2
PACK = 16
WIDTH = 120
BLOCK = 30
FETCHES = (0, 30, 90, 150, 240, 330)
ROW_BLOCK = 256
VMEM_LIMIT = 40 * 1024 * 1024
SMALL_LIMIT = 16 * 1024 * 1024
FULL_LIMIT = 59 * 1024 * 1024


def spans(cols):
    return [(q * WIDTH, min(cols, (q + 1) * WIDTH)) for q in range(QUARTERS)]


def contribute_kernel(
    source, tile, dest, state, weight, out, blocks, loose, picks, product, turned, ready, sems, sent
):
    levels, rows, cols = state.shape
    entries = weight.shape[1]
    per_quarter = WIDTH // BLOCK
    groups = entries // PACK
    steps = -(-cols // BLOCK)
    lane = lax.broadcasted_iota(jnp.int32, (1, LANES), 1)

    fetches = {}
    for number, (low, high) in enumerate(zip(FETCHES, FETCHES[1:] + (cols,))):
        span = pl.ds(low, high - low)
        fetches[low] = pltpu.make_async_copy(weight.at[span], blocks.at[span], sems.at[number])
        fetches[low].start()

    place = lax.broadcasted_iota(jnp.int32, (entries, rows), 0)
    wanted = jnp.zeros((entries, rows), jnp.int32)
    for entry in range(entries):
        wanted = jnp.where(place == entry, source[entry], wanted)
    onehot = jnp.where(wanted == lax.broadcasted_iota(jnp.int32, (entries, rows), 1), 1.0, 0.0)
    onehot = onehot.astype(jnp.bfloat16)
    below = lax.broadcasted_iota(jnp.int32, (8, LANES), 0)
    here = lax.broadcasted_iota(jnp.int32, (8, LANES), 1) % 8
    for slot in range(2 * groups):
        tiles = jnp.zeros((8, LANES), jnp.int32)
        dests = jnp.zeros((8, LANES), jnp.int32)
        for e in range(8):
            tiles = jnp.where(here == e, tile[slot * 8 + e], tiles)
            dests = jnp.where(here == e, dest[slot * 8 + e], dests)
        tail = jnp.where(below == 6, tiles, jnp.where(below == 7, dests, 0))
        turned[WIDTH:LANES, slot * LANES : (slot + 1) * LANES] = tail.astype(jnp.float32)
    for level in range(levels):
        picked = jnp.dot(onehot, state[level].astype(jnp.bfloat16), preferred_element_type=jnp.float32)
        for slot in range(2 * groups):
            loose[slot, level * 8 : level * 8 + 8, :] = picked[slot * 8 : slot * 8 + 8]
    for group in range(groups):
        for half in range(2):
            picks[group, half * LANES : (half + 1) * LANES, :] = loose[2 * group + half].astype(jnp.bfloat16)

    sends = []
    for step in range(steps):
        if step * BLOCK in fetches:
            fetches[step * BLOCK].wait()
        base = (step % per_quarter) * BLOCK
        for group in range(groups):
            streamed = blocks[step * BLOCK : (step + 1) * BLOCK, group * PACK : (group + 1) * PACK, :]
            whole = lax.dot_general(
                streamed.reshape(BLOCK * PACK, cols),
                picks[group],
                (((1,), (1,)), ((), ())),
                preferred_element_type=jnp.float32,
            ).reshape(BLOCK, PACK, 2 * LANES)
            for half in range(2):
                slot = 2 * group + half
                own = whole[:, half * 8 : half * 8 + 8, half * LANES : (half + 1) * LANES]
                product[slot] = own.reshape(BLOCK * 8, LANES)
                y = jnp.zeros((BLOCK, LANES), jnp.float32)
                for e in range(8):
                    y = jnp.where(lane % 8 == e, product[slot, pl.ds(e, BLOCK, stride=8), :], y)
                if (step + 1) * BLOCK > cols:
                    column = lax.broadcasted_iota(jnp.int32, (BLOCK, LANES), 0) + step * BLOCK
                    y = jnp.where(column < cols, y, 0.0)
                turned[base : base + BLOCK, slot * LANES : (slot + 1) * LANES] = y
        if step % per_quarter == per_quarter - 1 or step == steps - 1:
            quarter = step // per_quarter
            for slot in range(2 * groups):
                block = turned[:, slot * LANES : (slot + 1) * LANES].T
                for level in range(levels):
                    ready[quarter, level, slot * 8 : slot * 8 + 8, :] = block[level * 8 : level * 8 + 8]
            sends.append(pltpu.make_async_copy(ready.at[quarter], out.at[:, quarter], sent.at[quarter]))
            sends[-1].start()
    for send in sends:
        send.wait()


def contribute(state, weight, source, tile, dest):
    levels, rows, cols = state.shape
    entries = weight.shape[1]
    groups = entries // PACK
    steps = -(-cols // BLOCK)
    scalars = pl.BlockSpec(memory_space=pltpu.SMEM)
    away = pl.BlockSpec(memory_space=pltpu.HBM)
    return pl.pallas_call(
        contribute_kernel,
        in_specs=[scalars, scalars, scalars, pl.BlockSpec(memory_space=pltpu.VMEM), away],
        out_specs=away,
        scratch_shapes=[
            pltpu.VMEM((steps * BLOCK, entries, cols), jnp.bfloat16),
            pltpu.VMEM((2 * groups, LANES, cols), jnp.float32),
            pltpu.VMEM((groups, 2 * LANES, cols), jnp.bfloat16),
            pltpu.VMEM((2 * groups, BLOCK * 8, LANES), jnp.float32),
            pltpu.VMEM((LANES, 2 * groups * LANES), jnp.float32),
            pltpu.VMEM((QUARTERS, levels, entries, LANES), jnp.float32),
            pltpu.SemaphoreType.DMA((len(FETCHES),)),
            pltpu.SemaphoreType.DMA((QUARTERS,)),
        ],
        out_shape=jax.ShapeDtypeStruct((levels, QUARTERS, entries, LANES), jnp.float32),
        compiler_params=pltpu.CompilerParams(vmem_limit_bytes=VMEM_LIMIT),
        cost_estimate=pl.CostEstimate(
            flops=2 * entries * levels * cols * cols,
            bytes_accessed=2 * entries * cols * cols,
            transcendentals=0,
        ),
        name="contribute",
    )(source, tile, dest, state, weight)


def gather_rows_kernel(tile_rows, values, out, halves, labels):
    count = values.shape[0]
    x = values[...]
    high = x.astype(jnp.bfloat16)
    halves[:, :LANES] = high
    halves[:, LANES:] = (x - high.astype(jnp.float32)).astype(jnp.bfloat16)
    lane = lax.broadcasted_iota(jnp.int32, (8, LANES), 1)
    pick = jnp.where(lane == LANES - 2, float(tile_rows), jnp.where(lane == LANES - 1, 1.0, 0.0))
    labels[...] = lax.dot_general(
        pick.astype(jnp.bfloat16), high, (((1,), (1,)), ((), ())), preferred_element_type=jnp.float32
    ).astype(jnp.int32)
    for block in range(out.shape[0] // ROW_BLOCK):
        row = lax.broadcasted_iota(jnp.int32, (ROW_BLOCK, count), 0) + block * ROW_BLOCK
        onehot = jnp.where(row == labels[0:1, :], 1.0, 0.0).astype(jnp.bfloat16)
        both = jnp.dot(onehot, halves[...], preferred_element_type=jnp.float32)
        out[block * ROW_BLOCK : (block + 1) * ROW_BLOCK, :] = both[:, :LANES] + both[:, LANES:]


def gather_rows(values, tiles, tile_rows):
    count = values.shape[0]
    return pl.pallas_call(
        functools.partial(gather_rows_kernel, tile_rows),
        in_specs=[pl.BlockSpec(memory_space=pltpu.VMEM)],
        out_specs=pl.BlockSpec(memory_space=pltpu.VMEM),
        out_shape=jax.ShapeDtypeStruct((tiles * tile_rows, LANES), jnp.float32),
        scratch_shapes=[
            pltpu.VMEM((count, 2 * LANES), jnp.bfloat16),
            pltpu.VMEM((8, count), jnp.int32),
        ],
        compiler_params=pltpu.CompilerParams(vmem_limit_bytes=VMEM_LIMIT),
        name="gather_rows",
    )(values)


def coefficient(flags, diffusion, mask):
    return diffusion * jnp.where(flags[0] == 1, mask.astype(jnp.float32), 1.0)


def edges_kernel(first, last, bottom, diffusion, low, high):
    levels, rows, _ = first.shape
    cols = diffusion.shape[1]
    end = (cols - 2) % LANES
    starts = [first[level][:, :2] for level in range(levels)] + [diffusion[:, :2]]
    ends = [last[level][:, end : end + 2] for level in range(levels)] + [diffusion[:, cols - 2 :]]
    edge = jnp.concatenate([bottom[level, 7:8, :] for level in range(levels)], axis=0)
    for out, pairs in ((low, starts), (high, ends)):
        message = jnp.concatenate(pairs, axis=1)
        out[:levels, :cols] = edge
        for part in range(rows // 8):
            start = part * LANES
            out[levels:, start : start + message.shape[1]] = message[part * 8 : part * 8 + 8]


def edges(field, diffusion):
    levels, rows, cols = field.shape
    out = jax.ShapeDtypeStruct((levels + 8, rows // 8 * LANES), jnp.float32)
    message = pl.BlockSpec(out.shape, lambda i: (0, 0))
    return pl.pallas_call(
        edges_kernel,
        grid=(1,),
        in_specs=[
            pl.BlockSpec((levels, rows, LANES), lambda i: (0, 0, 0)),
            pl.BlockSpec((levels, rows, LANES), lambda i: (0, 0, (cols - 2) // LANES)),
            pl.BlockSpec((levels, 8, cols), lambda i: (0, rows // 8 - 1, 0)),
            pl.BlockSpec((rows, cols), lambda i: (0, 0)),
        ],
        out_specs=[message, message],
        out_shape=[out, out],
        compiler_params=pltpu.CompilerParams(vmem_limit_bytes=FULL_LIMIT),
        name="edges",
    )(field, field, field, diffusion)


def columns(message, rows):
    tall = message.shape[0]
    parts = [message[tall - 8 :, part * LANES : (part + 1) * LANES] for part in range(rows // 8)]
    return jnp.concatenate(parts, axis=0)


def rims_kernel(first, last, diffusion, west, east, low, high, three, sides):
    levels, _, cols = first.shape
    rows = diffusion.shape[0]
    left, right = columns(west, rows), columns(east, rows)
    sides[0] = left
    sides[1] = right
    low[...] = jnp.zeros(low.shape, jnp.float32)
    high[...] = jnp.zeros(high.shape, jnp.float32)
    for out, block, start in ((low, first, 0), (high, last, rows - 2)):
        for level in range(levels + 1):
            place = pl.ds(2 * level, 2)
            if level < levels:
                out[place, SIDE : SIDE + cols] = block[level, start % 8 : start % 8 + 2, :]
            else:
                out[place, SIDE : SIDE + cols] = diffusion[start : start + 2, :]
            out[place, SIDE - 2 : SIDE] = left[start : start + 2, 2 * level : 2 * level + 2]
            out[place, SIDE + cols : SIDE + cols + 2] = right[start : start + 2, 2 * level : 2 * level + 2]
    three[0] = west[:levels, :cols]
    three[1] = jnp.concatenate([last[level, 7:8, :] for level in range(levels)], axis=0)
    three[2] = east[:levels, :cols]


def rims(field, diffusion, west, east):
    levels, rows, cols = field.shape
    wide = LANES * -(-(cols + 2 * SIDE) // LANES)
    rim = jax.ShapeDtypeStruct((2 * levels + 2, wide), jnp.float32)
    three = jax.ShapeDtypeStruct((3, levels, cols), jnp.float32)
    sides = jax.ShapeDtypeStruct((2, rows, LANES), jnp.float32)
    whole = lambda shape: pl.BlockSpec(shape, lambda i: (0,) * len(shape))
    return pl.pallas_call(
        rims_kernel,
        grid=(1,),
        in_specs=[
            pl.BlockSpec((levels, 8, cols), lambda i: (0, 0, 0)),
            pl.BlockSpec((levels, 8, cols), lambda i: (0, rows // 8 - 1, 0)),
            whole((rows, cols)),
            whole(west.shape),
            whole(east.shape),
        ],
        out_specs=[whole(rim.shape), whole(rim.shape), whole(three.shape), whole(sides.shape)],
        out_shape=[rim, rim, three, sides],
        compiler_params=pltpu.CompilerParams(vmem_limit_bytes=FULL_LIMIT),
        name="rims",
    )(field, field, diffusion, west, east)


def mix_kernel(
    flags, field, diffusion, rate, mask, sides, south, north, near, behind, ahead, fold_map, out, ext, coefs, folded
):
    levels, rows, cols = field.shape
    own_rows, own_lanes = slice(8, 8 + rows), slice(SIDE, SIDE + cols)
    active = coefficient(flags, 1.0, mask[...])
    pull = rate[...] * active
    ext[...] = jnp.zeros(ext.shape, jnp.float32)
    coefs[...] = jnp.zeros(coefs.shape, jnp.float32)
    coefs[own_rows, own_lanes] = diffusion[...] * active
    coefs[own_rows, SIDE - 2 : SIDE] = sides[0, :, 2 * levels : 2 * levels + 2]
    coefs[own_rows, SIDE + cols : SIDE + cols + 2] = sides[1, :, 2 * levels : 2 * levels + 2]
    coefs[6:8, :] = south[2 * levels : 2 * levels + 2, :]
    coefs[8 + rows : 10 + rows, :] = north[2 * levels : 2 * levels + 2, :]

    @pl.when(flags[1] == 1)
    def fold():
        total = jnp.zeros((3 * levels, cols), jnp.float32)
        place = lax.broadcasted_iota(jnp.int32, (cols, cols), 0)
        held = [behind[1], behind[2], near[0], near[1], near[2], ahead[0], ahead[1], ahead[2]]
        for number, whole in enumerate(held):
            copy = (flags[2] + number + 5) % 8
            high = whole.astype(jnp.bfloat16).astype(jnp.float32)
            rest = whole - high
            middle = rest.astype(jnp.bfloat16).astype(jnp.float32)
            parts = jnp.concatenate([high, middle, rest - middle], axis=0).astype(jnp.bfloat16)
            onehot = jnp.where(place + copy * cols == fold_map[...], 1.0, 0.0).astype(jnp.bfloat16)
            total = total + jnp.dot(parts, onehot, preferred_element_type=jnp.float32)
        folded[...] = total[:levels] + total[levels : 2 * levels] + total[2 * levels :]

    tall, wide = ext.shape[1:]
    again = jnp.where(flags[0] == 1, 0.0, 1.0)

    def sweep(f, c):
        around = pltpu.roll(f, 1, 0) + pltpu.roll(f, tall - 1, 0)
        around = around + pltpu.roll(f, 1, 1) + pltpu.roll(f, wide - 1, 1)
        return f + c * (around - 4.0 * f)

    for level in range(levels):
        pair = slice(2 * level, 2 * level + 2)
        ext[level, own_rows, own_lanes] = field[level]
        ext[level, own_rows, SIDE - 2 : SIDE] = sides[0, :, pair]
        ext[level, own_rows, SIDE + cols : SIDE + cols + 2] = sides[1, :, pair]
        ext[level, 6:8, :] = south[pair, :]
        ext[level, 8 + rows : 10 + rows, :] = north[pair, :]

    @pl.when(flags[1] == 1)
    def folded_rows():
        for level in range(levels):
            ext[level, 8 + rows : 9 + rows, own_lanes] = folded[level : level + 1, :]

    for level in range(levels):
        once = sweep(ext[level], coefs[...])
        twice = sweep(once, coefs[...] * again)
        out[level] = twice[own_rows, own_lanes] - pull * field[level]


def mix(flags, field, diffusion, rate, mask, sides, south, north, near, behind, ahead, fold_map):
    levels, rows, cols = field.shape
    wide = south.shape[1]
    inside = pl.BlockSpec(memory_space=pltpu.VMEM)
    return pl.pallas_call(
        mix_kernel,
        in_specs=[pl.BlockSpec(memory_space=pltpu.SMEM)] + [inside] * 11,
        out_specs=inside,
        scratch_shapes=[
            pltpu.VMEM((levels, rows + 16, wide), jnp.float32),
            pltpu.VMEM((rows + 16, wide), jnp.float32),
            pltpu.VMEM((levels, cols), jnp.float32),
        ],
        out_shape=jax.ShapeDtypeStruct(field.shape, jnp.float32),
        compiler_params=pltpu.CompilerParams(vmem_limit_bytes=SMALL_LIMIT),
        name="mix",
    )(flags, field, diffusion, rate, mask, sides, south, north, near, behind, ahead, fold_map[None])


def finish_kernel(flags, received, base, rate, mask, out, outer, stored):
    levels, rows, cols = base.shape
    parts = stored.shape[0]
    part = levels // parts
    pull = coefficient(flags, rate[...], mask[...])
    stores = []
    for number in range(parts):
        for level in range(number * part, (number + 1) * part):
            pieces = [received[level * QUARTERS + q][:, : high - low] for q, (low, high) in enumerate(spans(cols))]
            outer[level] = base[level] + pull * jnp.concatenate(pieces, axis=1)
        span = pl.ds(number * part, part)
        stores.append(pltpu.make_async_copy(outer.at[span], out.at[span], stored.at[number]))
        stores[-1].start()
    for store in stores:
        store.wait()


def finish(flags, received, base, rate, mask):
    parts = 4
    inside = pl.BlockSpec(memory_space=pltpu.VMEM)
    return pl.pallas_call(
        finish_kernel,
        in_specs=[pl.BlockSpec(memory_space=pltpu.SMEM), inside, inside, inside, inside],
        out_specs=pl.BlockSpec(memory_space=pltpu.HBM),
        out_shape=jax.ShapeDtypeStruct(base.shape, jnp.float32),
        scratch_shapes=[pltpu.VMEM(base.shape, jnp.float32), pltpu.SemaphoreType.DMA((parts,))],
        compiler_params=pltpu.CompilerParams(vmem_limit_bytes=SMALL_LIMIT),
        name="finish",
    )(flags, received, base, rate, mask)


def shift(value, axis, forward, periodic):
    count = lax.axis_size(axis)
    pairs = [(i, i + 1) for i in range(count - 1)] + ([(count - 1, 0)] if periodic else [])
    if not forward:
        pairs = [(b, a) for a, b in pairs]
    return lax.ppermute(value, axis, pairs)


def across(value, distance):
    count = lax.axis_size("ty")
    start = 2 * lax.axis_size("tx") * count - count
    pairs = [(start + i, start + (i + distance) % count) for i in range(count)]
    return lax.ppermute(value, ("mp", "tx", "ty"), pairs)


def spread(value, axes):
    return lax.all_to_all(value, axes, split_axis=0, concat_axis=0, tiled=True)


def body(
    state,
    diffusion,
    exchange_rate,
    land_mask,
    fold_map,
    entry_tile,
    entry_source,
    entry_dest,
    entry_weight,
):
    field = state[0]
    levels, rows, cols = field.shape
    tiles = lax.axis_size("tx") * lax.axis_size("ty")
    entries = entry_source.shape[2]
    ocean = lax.axis_index("mp") == 1
    fold_here = jnp.logical_and(ocean, lax.axis_index("tx") == lax.axis_size("tx") - 1)
    flags = jnp.stack([ocean, fold_here, lax.axis_index("ty")]).astype(jnp.int32)
    low, high = edges(field, diffusion[0])
    west = shift(high, "ty", True, True)
    east = shift(low, "ty", False, True)

    source, tile, dest = entry_source[0, 0], entry_tile[0, 0, :, 0], entry_dest[0, 0]
    weight = jnp.transpose(entry_weight[0, 0], (1, 0, 2))
    pieces = contribute(field, weight, source, tile, dest)
    pieces, west, east = lax.optimization_barrier((pieces, west, east))
    arrived = spread(pieces.reshape(tiles, entries, LANES), TILE_AXES)

    low, high, near, sides = rims(field, diffusion[0], west, east)
    south = shift(high, "tx", True, False)
    north = shift(low, "tx", False, False)
    behind = across(near, 3)
    ahead = across(near, -3)
    summed = gather_rows(arrived.reshape(-1, LANES), tiles, rows).reshape(tiles, rows, LANES)
    summed, south, north, behind, ahead = lax.optimization_barrier((summed, south, north, behind, ahead))
    base = mix(
        flags,
        field,
        diffusion[0],
        exchange_rate[0],
        land_mask,
        sides,
        south,
        north,
        near,
        behind,
        ahead,
        fold_map,
    )
    received, base = lax.optimization_barrier((spread(summed, TILE_AXES), base))
    received = lax.ppermute(received, "mp", [(0, 1), (1, 0)])
    return finish(flags, received, base, exchange_rate[0], land_mask)[None]


def solution(mesh):
    in_specs = (
        P("mp", None, "tx", "ty"),
        P("mp", "tx", "ty"),
        P("mp", "tx", "ty"),
        P("tx", "ty"),
        P("ty"),
        P("mp", "tx", "ty", None),
        P("mp", "tx", "ty"),
        P("mp", "tx", "ty"),
        P("mp", "tx", "ty", None, None),
    )
    out_specs = P("mp", None, "tx", "ty")
    return jax.shard_map(body, mesh=mesh, in_specs=in_specs, out_specs=out_specs, check_vma=False)
```

```python
import functools

import jax
import jax.numpy as jnp
from jax import lax
from jax.experimental import pallas as pl
from jax.experimental.pallas import tpu as pltpu
from jax.sharding import PartitionSpec as P

TILE_AXES = ("tx", "ty")
QUARTERS = 4
LANES = 128
SIDE = 2
PACK = 16
WIDTH = 120
BLOCK = 30
FETCHES = (0, 30, 90, 150, 240, 330)
ROW_BLOCK = 256
VMEM_LIMIT = 40 * 1024 * 1024
SMALL_LIMIT = 16 * 1024 * 1024
FULL_LIMIT = 59 * 1024 * 1024


def spans(cols):
    return [(q * WIDTH, min(cols, (q + 1) * WIDTH)) for q in range(QUARTERS)]


def contribute_kernel(
    source, tile, dest, state, weight, out, blocks, loose, picks, product, turned, ready, sems, sent
):
    levels, rows, cols = state.shape
    entries = weight.shape[1]
    per_quarter = WIDTH // BLOCK
    groups = entries // PACK
    steps = -(-cols // BLOCK)
    lane = lax.broadcasted_iota(jnp.int32, (1, LANES), 1)

    fetches = {}
    for number, (low, high) in enumerate(zip(FETCHES, FETCHES[1:] + (cols,))):
        span = pl.ds(low, high - low)
        fetches[low] = pltpu.make_async_copy(weight.at[span], blocks.at[span], sems.at[number])
        fetches[low].start()

    place = lax.broadcasted_iota(jnp.int32, (entries, rows), 0)
    wanted = jnp.zeros((entries, rows), jnp.int32)
    for entry in range(entries):
        wanted = jnp.where(place == entry, source[entry], wanted)
    onehot = jnp.where(wanted == lax.broadcasted_iota(jnp.int32, (entries, rows), 1), 1.0, 0.0)
    onehot = onehot.astype(jnp.bfloat16)
    below = lax.broadcasted_iota(jnp.int32, (8, LANES), 0)
    here = lax.broadcasted_iota(jnp.int32, (8, LANES), 1) % 8
    for slot in range(2 * groups):
        tiles = jnp.zeros((8, LANES), jnp.int32)
        dests = jnp.zeros((8, LANES), jnp.int32)
        for e in range(8):
            tiles = jnp.where(here == e, tile[slot * 8 + e], tiles)
            dests = jnp.where(here == e, dest[slot * 8 + e], dests)
        tail = jnp.where(below == 6, tiles, jnp.where(below == 7, dests, 0))
        turned[WIDTH:LANES, slot * LANES : (slot + 1) * LANES] = tail.astype(jnp.float32)
    for level in range(levels):
        picked = jnp.dot(onehot, state[level].astype(jnp.bfloat16), preferred_element_type=jnp.float32)
        for slot in range(2 * groups):
            loose[slot, level * 8 : level * 8 + 8, :] = picked[slot * 8 : slot * 8 + 8]
    for group in range(groups):
        for half in range(2):
            picks[group, half * LANES : (half + 1) * LANES, :] = loose[2 * group + half].astype(jnp.bfloat16)

    sends = []
    for step in range(steps):
        if step * BLOCK in fetches:
            fetches[step * BLOCK].wait()
        base = (step % per_quarter) * BLOCK
        for group in range(groups):
            streamed = blocks[step * BLOCK : (step + 1) * BLOCK, group * PACK : (group + 1) * PACK, :]
            whole = lax.dot_general(
                streamed.reshape(BLOCK * PACK, cols),
                picks[group],
                (((1,), (1,)), ((), ())),
                preferred_element_type=jnp.float32,
            ).reshape(BLOCK, PACK, 2 * LANES)
            for half in range(2):
                slot = 2 * group + half
                own = whole[:, half * 8 : half * 8 + 8, half * LANES : (half + 1) * LANES]
                product[slot] = own.reshape(BLOCK * 8, LANES)
                y = jnp.zeros((BLOCK, LANES), jnp.float32)
                for e in range(8):
                    y = jnp.where(lane % 8 == e, product[slot, pl.ds(e, BLOCK, stride=8), :], y)
                if (step + 1) * BLOCK > cols:
                    column = lax.broadcasted_iota(jnp.int32, (BLOCK, LANES), 0) + step * BLOCK
                    y = jnp.where(column < cols, y, 0.0)
                turned[base : base + BLOCK, slot * LANES : (slot + 1) * LANES] = y
        if step % per_quarter == per_quarter - 1 or step == steps - 1:
            quarter = step // per_quarter
            for slot in range(2 * groups):
                block = turned[:, slot * LANES : (slot + 1) * LANES].T
                for level in range(levels):
                    ready[quarter, level, slot * 8 : slot * 8 + 8, :] = block[level * 8 : level * 8 + 8]
            sends.append(pltpu.make_async_copy(ready.at[quarter], out.at[:, quarter], sent.at[quarter]))
            sends[-1].start()
    for send in sends:
        send.wait()


def contribute(state, weight, source, tile, dest):
    levels, rows, cols = state.shape
    entries = weight.shape[1]
    groups = entries // PACK
    steps = -(-cols // BLOCK)
    scalars = pl.BlockSpec(memory_space=pltpu.SMEM)
    away = pl.BlockSpec(memory_space=pltpu.HBM)
    return pl.pallas_call(
        contribute_kernel,
        in_specs=[scalars, scalars, scalars, pl.BlockSpec(memory_space=pltpu.VMEM), away],
        out_specs=away,
        scratch_shapes=[
            pltpu.VMEM((steps * BLOCK, entries, cols), jnp.bfloat16),
            pltpu.VMEM((2 * groups, LANES, cols), jnp.float32),
            pltpu.VMEM((groups, 2 * LANES, cols), jnp.bfloat16),
            pltpu.VMEM((2 * groups, BLOCK * 8, LANES), jnp.float32),
            pltpu.VMEM((LANES, 2 * groups * LANES), jnp.float32),
            pltpu.VMEM((QUARTERS, levels, entries, LANES), jnp.float32),
            pltpu.SemaphoreType.DMA((len(FETCHES),)),
            pltpu.SemaphoreType.DMA((QUARTERS,)),
        ],
        out_shape=jax.ShapeDtypeStruct((levels, QUARTERS, entries, LANES), jnp.float32),
        compiler_params=pltpu.CompilerParams(vmem_limit_bytes=VMEM_LIMIT),
        cost_estimate=pl.CostEstimate(
            flops=2 * entries * levels * cols * cols,
            bytes_accessed=2 * entries * cols * cols,
            transcendentals=0,
        ),
        name="contribute",
    )(source, tile, dest, state, weight)


def gather_rows_kernel(tile_rows, values, out, halves, labels, sums, stored):
    count = values.shape[0]
    x = values[...]
    high = x.astype(jnp.bfloat16)
    halves[:, :LANES] = high
    halves[:, LANES:] = (x - high.astype(jnp.float32)).astype(jnp.bfloat16)
    lane = lax.broadcasted_iota(jnp.int32, (8, LANES), 1)
    pick = jnp.where(lane == LANES - 2, float(tile_rows), jnp.where(lane == LANES - 1, 1.0, 0.0))
    labels[...] = lax.dot_general(
        pick.astype(jnp.bfloat16), high, (((1,), (1,)), ((), ())), preferred_element_type=jnp.float32
    ).astype(jnp.int32)
    stores = []
    for block in range(out.shape[0] // ROW_BLOCK):
        row = lax.broadcasted_iota(jnp.int32, (ROW_BLOCK, count), 0) + block * ROW_BLOCK
        onehot = jnp.where(row == labels[0:1, :], 1.0, 0.0).astype(jnp.bfloat16)
        both = jnp.dot(onehot, halves[...], preferred_element_type=jnp.float32)
        span = pl.ds(block * ROW_BLOCK, ROW_BLOCK)
        sums[span, :] = both[:, :LANES] + both[:, LANES:]
        stores.append(pltpu.make_async_copy(sums.at[span], out.at[span], stored.at[block]))
        stores[-1].start()
    for store in stores:
        store.wait()


def gather_rows(values, tiles, tile_rows):
    count = values.shape[0]
    return pl.pallas_call(
        functools.partial(gather_rows_kernel, tile_rows),
        in_specs=[pl.BlockSpec(memory_space=pltpu.VMEM)],
        out_specs=pl.BlockSpec(memory_space=pltpu.HBM),
        out_shape=jax.ShapeDtypeStruct((tiles * tile_rows, LANES), jnp.float32),
        scratch_shapes=[
            pltpu.VMEM((count, 2 * LANES), jnp.bfloat16),
            pltpu.VMEM((8, count), jnp.int32),
            pltpu.VMEM((tiles * tile_rows, LANES), jnp.float32),
            pltpu.SemaphoreType.DMA((tiles * tile_rows // ROW_BLOCK,)),
        ],
        compiler_params=pltpu.CompilerParams(vmem_limit_bytes=VMEM_LIMIT),
        name="gather_rows",
    )(values)


def coefficient(flags, diffusion, mask):
    return diffusion * jnp.where(flags[0] == 1, mask.astype(jnp.float32), 1.0)


def edges_kernel(first, last, bottom, diffusion, low, high):
    levels, rows, _ = first.shape
    cols = diffusion.shape[1]
    end = (cols - 2) % LANES
    starts = [first[level][:, :2] for level in range(levels)] + [diffusion[:, :2]]
    ends = [last[level][:, end : end + 2] for level in range(levels)] + [diffusion[:, cols - 2 :]]
    edge = jnp.concatenate([bottom[level, 7:8, :] for level in range(levels)], axis=0)
    for out, pairs in ((low, starts), (high, ends)):
        message = jnp.concatenate(pairs, axis=1)
        out[:levels, :cols] = edge
        for part in range(rows // 8):
            start = part * LANES
            out[levels:, start : start + message.shape[1]] = message[part * 8 : part * 8 + 8]


def edges(field, diffusion):
    levels, rows, cols = field.shape
    out = jax.ShapeDtypeStruct((levels + 8, rows // 8 * LANES), jnp.float32)
    message = pl.BlockSpec(out.shape, lambda i: (0, 0))
    return pl.pallas_call(
        edges_kernel,
        grid=(1,),
        in_specs=[
            pl.BlockSpec((levels, rows, LANES), lambda i: (0, 0, 0)),
            pl.BlockSpec((levels, rows, LANES), lambda i: (0, 0, (cols - 2) // LANES)),
            pl.BlockSpec((levels, 8, cols), lambda i: (0, rows // 8 - 1, 0)),
            pl.BlockSpec((rows, cols), lambda i: (0, 0)),
        ],
        out_specs=[message, message],
        out_shape=[out, out],
        compiler_params=pltpu.CompilerParams(vmem_limit_bytes=FULL_LIMIT),
        name="edges",
    )(field, field, field, diffusion)


def columns(message, rows):
    tall = message.shape[0]
    parts = [message[tall - 8 :, part * LANES : (part + 1) * LANES] for part in range(rows // 8)]
    return jnp.concatenate(parts, axis=0)


def rims_kernel(first, last, diffusion, west, east, low, high, three, sides):
    levels, _, cols = first.shape
    rows = diffusion.shape[0]
    left, right = columns(west, rows), columns(east, rows)
    sides[0] = left
    sides[1] = right
    low[...] = jnp.zeros(low.shape, jnp.float32)
    high[...] = jnp.zeros(high.shape, jnp.float32)
    for out, block, start in ((low, first, 0), (high, last, rows - 2)):
        for level in range(levels + 1):
            place = pl.ds(2 * level, 2)
            if level < levels:
                out[place, SIDE : SIDE + cols] = block[level, start % 8 : start % 8 + 2, :]
            else:
                out[place, SIDE : SIDE + cols] = diffusion[start : start + 2, :]
            out[place, SIDE - 2 : SIDE] = left[start : start + 2, 2 * level : 2 * level + 2]
            out[place, SIDE + cols : SIDE + cols + 2] = right[start : start + 2, 2 * level : 2 * level + 2]
    three[0] = west[:levels, :cols]
    three[1] = jnp.concatenate([last[level, 7:8, :] for level in range(levels)], axis=0)
    three[2] = east[:levels, :cols]


def rims(field, diffusion, west, east):
    levels, rows, cols = field.shape
    wide = LANES * -(-(cols + 2 * SIDE) // LANES)
    rim = jax.ShapeDtypeStruct((2 * levels + 2, wide), jnp.float32)
    three = jax.ShapeDtypeStruct((3, levels, cols), jnp.float32)
    sides = jax.ShapeDtypeStruct((2, rows, LANES), jnp.float32)
    whole = lambda shape: pl.BlockSpec(shape, lambda i: (0,) * len(shape))
    return pl.pallas_call(
        rims_kernel,
        grid=(1,),
        in_specs=[
            pl.BlockSpec((levels, 8, cols), lambda i: (0, 0, 0)),
            pl.BlockSpec((levels, 8, cols), lambda i: (0, rows // 8 - 1, 0)),
            whole((rows, cols)),
            whole(west.shape),
            whole(east.shape),
        ],
        out_specs=[whole(rim.shape), whole(rim.shape), whole(three.shape), whole(sides.shape)],
        out_shape=[rim, rim, three, sides],
        compiler_params=pltpu.CompilerParams(vmem_limit_bytes=FULL_LIMIT),
        name="rims",
    )(field, field, diffusion, west, east)


def mix_kernel(
    flags, field, diffusion, rate, mask, sides, south, north, near, behind, ahead, fold_map, out, ext, coefs, folded
):
    levels, rows, cols = field.shape
    own_rows, own_lanes = slice(8, 8 + rows), slice(SIDE, SIDE + cols)
    active = coefficient(flags, 1.0, mask[...])
    pull = rate[...] * active
    ext[...] = jnp.zeros(ext.shape, jnp.float32)
    coefs[...] = jnp.zeros(coefs.shape, jnp.float32)
    coefs[own_rows, own_lanes] = diffusion[...] * active
    coefs[own_rows, SIDE - 2 : SIDE] = sides[0, :, 2 * levels : 2 * levels + 2]
    coefs[own_rows, SIDE + cols : SIDE + cols + 2] = sides[1, :, 2 * levels : 2 * levels + 2]
    coefs[6:8, :] = south[2 * levels : 2 * levels + 2, :]
    coefs[8 + rows : 10 + rows, :] = north[2 * levels : 2 * levels + 2, :]

    @pl.when(flags[1] == 1)
    def fold():
        total = jnp.zeros((3 * levels, cols), jnp.float32)
        place = lax.broadcasted_iota(jnp.int32, (cols, cols), 0)
        held = [behind[1], behind[2], near[0], near[1], near[2], ahead[0], ahead[1], ahead[2]]
        for number, whole in enumerate(held):
            copy = (flags[2] + number + 5) % 8
            high = whole.astype(jnp.bfloat16).astype(jnp.float32)
            rest = whole - high
            middle = rest.astype(jnp.bfloat16).astype(jnp.float32)
            parts = jnp.concatenate([high, middle, rest - middle], axis=0).astype(jnp.bfloat16)
            onehot = jnp.where(place + copy * cols == fold_map[...], 1.0, 0.0).astype(jnp.bfloat16)
            total = total + jnp.dot(parts, onehot, preferred_element_type=jnp.float32)
        folded[...] = total[:levels] + total[levels : 2 * levels] + total[2 * levels :]

    tall, wide = ext.shape[1:]
    again = jnp.where(flags[0] == 1, 0.0, 1.0)

    def sweep(f, c):
        around = pltpu.roll(f, 1, 0) + pltpu.roll(f, tall - 1, 0)
        around = around + pltpu.roll(f, 1, 1) + pltpu.roll(f, wide - 1, 1)
        return f + c * (around - 4.0 * f)

    for level in range(levels):
        pair = slice(2 * level, 2 * level + 2)
        ext[level, own_rows, own_lanes] = field[level]
        ext[level, own_rows, SIDE - 2 : SIDE] = sides[0, :, pair]
        ext[level, own_rows, SIDE + cols : SIDE + cols + 2] = sides[1, :, pair]
        ext[level, 6:8, :] = south[pair, :]
        ext[level, 8 + rows : 10 + rows, :] = north[pair, :]

    @pl.when(flags[1] == 1)
    def folded_rows():
        for level in range(levels):
            ext[level, 8 + rows : 9 + rows, own_lanes] = folded[level : level + 1, :]

    for level in range(levels):
        once = sweep(ext[level], coefs[...])
        twice = sweep(once, coefs[...] * again)
        out[level] = twice[own_rows, own_lanes] - pull * field[level]


def mix(flags, field, diffusion, rate, mask, sides, south, north, near, behind, ahead, fold_map):
    levels, rows, cols = field.shape
    wide = south.shape[1]
    inside = pl.BlockSpec(memory_space=pltpu.VMEM)
    return pl.pallas_call(
        mix_kernel,
        in_specs=[pl.BlockSpec(memory_space=pltpu.SMEM)] + [inside] * 11,
        out_specs=inside,
        scratch_shapes=[
            pltpu.VMEM((levels, rows + 16, wide), jnp.float32),
            pltpu.VMEM((rows + 16, wide), jnp.float32),
            pltpu.VMEM((levels, cols), jnp.float32),
        ],
        out_shape=jax.ShapeDtypeStruct(field.shape, jnp.float32),
        compiler_params=pltpu.CompilerParams(vmem_limit_bytes=SMALL_LIMIT),
        name="mix",
    )(flags, field, diffusion, rate, mask, sides, south, north, near, behind, ahead, fold_map[None])


def finish_kernel(flags, received, base, rate, mask, out, outer, stored):
    levels, rows, cols = base.shape
    parts = stored.shape[0]
    part = levels // parts
    pull = coefficient(flags, rate[...], mask[...])
    stores = []
    for number in range(parts):
        for level in range(number * part, (number + 1) * part):
            pieces = [received[level * QUARTERS + q][:, : high - low] for q, (low, high) in enumerate(spans(cols))]
            outer[level] = base[level] + pull * jnp.concatenate(pieces, axis=1)
        span = pl.ds(number * part, part)
        stores.append(pltpu.make_async_copy(outer.at[span], out.at[span], stored.at[number]))
        stores[-1].start()
    for store in stores:
        store.wait()


def finish(flags, received, base, rate, mask):
    parts = 4
    inside = pl.BlockSpec(memory_space=pltpu.VMEM)
    return pl.pallas_call(
        finish_kernel,
        in_specs=[pl.BlockSpec(memory_space=pltpu.SMEM), inside, inside, inside, inside],
        out_specs=pl.BlockSpec(memory_space=pltpu.HBM),
        out_shape=jax.ShapeDtypeStruct(base.shape, jnp.float32),
        scratch_shapes=[pltpu.VMEM(base.shape, jnp.float32), pltpu.SemaphoreType.DMA((parts,))],
        compiler_params=pltpu.CompilerParams(vmem_limit_bytes=SMALL_LIMIT),
        name="finish",
    )(flags, received, base, rate, mask)


def shift(value, axis, forward, periodic):
    count = lax.axis_size(axis)
    pairs = [(i, i + 1) for i in range(count - 1)] + ([(count - 1, 0)] if periodic else [])
    if not forward:
        pairs = [(b, a) for a, b in pairs]
    return lax.ppermute(value, axis, pairs)


def across(value, distance):
    count = lax.axis_size("ty")
    start = 2 * lax.axis_size("tx") * count - count
    pairs = [(start + i, start + (i + distance) % count) for i in range(count)]
    return lax.ppermute(value, ("mp", "tx", "ty"), pairs)


def spread(value, axes):
    return lax.all_to_all(value, axes, split_axis=0, concat_axis=0, tiled=True)


def body(
    state,
    diffusion,
    exchange_rate,
    land_mask,
    fold_map,
    entry_tile,
    entry_source,
    entry_dest,
    entry_weight,
):
    field = state[0]
    levels, rows, cols = field.shape
    tiles = lax.axis_size("tx") * lax.axis_size("ty")
    entries = entry_source.shape[2]
    ocean = lax.axis_index("mp") == 1
    fold_here = jnp.logical_and(ocean, lax.axis_index("tx") == lax.axis_size("tx") - 1)
    flags = jnp.stack([ocean, fold_here, lax.axis_index("ty")]).astype(jnp.int32)
    low, high = edges(field, diffusion[0])
    west = shift(high, "ty", True, True)
    east = shift(low, "ty", False, True)

    source, tile, dest = entry_source[0, 0], entry_tile[0, 0, :, 0], entry_dest[0, 0]
    weight = jnp.transpose(entry_weight[0, 0], (1, 0, 2))
    pieces = contribute(field, weight, source, tile, dest)
    pieces, west, east = lax.optimization_barrier((pieces, west, east))
    arrived = spread(pieces.reshape(tiles, entries, LANES), TILE_AXES)

    low, high, near, sides = rims(field, diffusion[0], west, east)
    south = shift(high, "tx", True, False)
    north = shift(low, "tx", False, False)
    behind = across(near, 3)
    ahead = across(near, -3)
    summed = gather_rows(arrived.reshape(-1, LANES), tiles, rows).reshape(tiles, rows, LANES)
    summed, south, north, behind, ahead = lax.optimization_barrier((summed, south, north, behind, ahead))
    base = mix(
        flags,
        field,
        diffusion[0],
        exchange_rate[0],
        land_mask,
        sides,
        south,
        north,
        near,
        behind,
        ahead,
        fold_map,
    )
    received, base = lax.optimization_barrier((spread(summed, TILE_AXES), base))
    received = lax.ppermute(received, "mp", [(0, 1), (1, 0)])
    return finish(flags, received, base, exchange_rate[0], land_mask)[None]


def solution(mesh):
    in_specs = (
        P("mp", None, "tx", "ty"),
        P("mp", "tx", "ty"),
        P("mp", "tx", "ty"),
        P("tx", "ty"),
        P("ty"),
        P("mp", "tx", "ty", None),
        P("mp", "tx", "ty"),
        P("mp", "tx", "ty"),
        P("mp", "tx", "ty", None, None),
    )
    out_specs = P("mp", None, "tx", "ty")
    return jax.shard_map(body, mesh=mesh, in_specs=in_specs, out_specs=out_specs, check_vma=False)
```
